128 devices in a mesh: dp: 32 (over y, z, core), mp: 4 (over x).
Axes of the slice: x: 4, y: 4, z: 4, core: 2. Of those that a mesh axis runs over, the one named last changes fastest.
Arguments:
- prompt_hidden: bfloat16 [4096, 5120], P('dp'), may hold values from -6 to 6
- kv_weight: bfloat16 [5120, 2, 1024], P(None, None, 'mp'), may hold values from -0.078125 to 0.078125
- queries: bfloat16 [256, 128, 5120], P('dp', None, 'mp'), may hold values from -88 to 88
- out_grad: bfloat16 [256, 128, 5120], P('dp', None, 'mp'), may hold values from -6 to 6
- own_kv: bfloat16 [256, 128, 2, 1024], P('dp', None, None, 'mp'), may hold values from -4 to 4
- pack_counts: int32 [32], replicated, may hold values from 0 to 8, as said below
- slot_groups: int32 [32, 8], replicated, may hold values from 0 to 7, as said below
- block_group: int32 [32], replicated, may hold values from 0 to 7, as said below
Outputs:
- attn_out: bfloat16 [256, 128, 5120], P('dp', None, 'mp')
- query_grad: bfloat16 [256, 128, 5120], P('dp', None, 'mp')
- own_kv_grad: bfloat16 [256, 128, 2, 1024], P('dp', None, None, 'mp')
- weight_grad: float32 [5120, 2, 1024], P('dp', None, 'mp')
- prompt_grad: bfloat16 [4096, 5120], P('dp', 'mp')
The draws below stay inside these ranges and needn't reach their ends.
Inputs may be any that keep to these rules, and one draw needn't show every extreme that they name: `pack_counts`: device d and device d + 16 together use 8 slots; some device uses all 8. `slot_groups`: used slots name every prompt exactly 16 times; unused slots hold arbitrary prompt numbers. `block_group`: every prompt has exactly 4 blocks.
All inputs are finite; a program needn't handle non-finite values.
Results may differ from the reference program's by a relative error of at most 0.028.
Values may be sent and summed in bfloat16 or wider, within the bound.
No kernel may reach another device: no remote copies, remote signals or barrier semaphores. Data moves between devices by JAX's collectives and lax.ppermute only.
A program may use at most 128 MiB of HBM per device.

```python
import math
import jax
import jax.numpy as jnp
from jax import lax

D = 5120
H = 40
KVH = 8
HD = 128
RESP = 128
PROMPT_DEV = 128
SLOTS = 8
GROUP = 16
GROUPS = 8
BLOCKS = 4
PROMPT = 512
N_DP = 32


def base_keys(key):
    raw_keys = jax.random.normal(key, (N_DP * SLOTS, RESP, 2, KVH * HD), jnp.float32)
    return jnp.clip(raw_keys, -4.0, 4.0)


def pair_counts(key):
    key = jax.random.fold_in(key, 101)
    half_count = N_DP // 2
    pair_loads = jax.random.randint(jax.random.fold_in(key, 1), (half_count,), 0, SLOTS + 1)
    chosen = jax.random.randint(jax.random.fold_in(key, 2), (), 0, half_count)
    pair_loads = jnp.where(jnp.arange(half_count) == chosen, SLOTS, pair_loads)
    flip_bits = jax.random.randint(jax.random.fold_in(key, 3), (half_count,), 0, 2)
    first_half = jnp.where(flip_bits == 1, pair_loads, SLOTS - pair_loads)
    return jnp.concatenate([first_half, SLOTS - first_half]).astype(jnp.int32)


def draw_pack_counts(key, part):
    pack_sizes = pair_counts(key)
    return pack_sizes


def draw_slot_groups(key, part):
    pack_sizes = pair_counts(key)
    key = jax.random.fold_in(key, 7)
    starts = jnp.cumsum(pack_sizes) - pack_sizes
    shuffled = jax.random.permutation(jax.random.fold_in(key, 1), GROUPS * GROUP)
    places = starts[:, None] + jnp.arange(SLOTS)[None, :]
    filled = jnp.arange(SLOTS)[None, :] < pack_sizes[:, None]
    named = shuffled[jnp.clip(places, 0, GROUPS * GROUP - 1)] // GROUP
    filler = jax.random.randint(jax.random.fold_in(key, 2), (N_DP, SLOTS), 0, GROUPS)
    return jnp.where(filled, named, filler).astype(jnp.int32)


def draw_block_group(key, part):
    key = jax.random.fold_in(key, 9)
    return (jax.random.permutation(key, N_DP) // BLOCKS).astype(jnp.int32)


def draw_own_kv(key, part):
    values_out = base_keys(key)
    return values_out.astype(jnp.bfloat16)


def draw_queries(key, part):
    key = jax.random.fold_in(key, 13)
    drawn = jnp.clip(jax.random.normal(key, (N_DP * SLOTS, RESP, H * HD), jnp.float32), -6.0, 6.0)
    return drawn.astype(jnp.bfloat16)


def spiked(drawn, own_key, source, target, blocks, factor):
    def block_of(axis_at):
        return (jnp.arange(drawn.shape[axis_at]) // (drawn.shape[axis_at] // blocks)).reshape((-1,) + (1,) * (drawn.ndim - 1 - axis_at))

    near = jax.random.permutation(own_key, blocks)[block_of(target)]
    second = (block_of(target) + blocks // 2) % blocks
    return jnp.where((block_of(source) == near) | (block_of(source) == second), factor * drawn, drawn)


def steps_of(own_key, dims, shards, smallest, high):
    def one(dim, parts):
        draws = jax.random.uniform(jax.random.fold_in(jax.random.fold_in(own_key, 6), dim), (parts,), jnp.float32, smallest / len(shards), high / len(shards))
        return jnp.repeat(jnp.exp(draws), dims[dim] // parts).reshape((-1,) + (1,) * (len(dims) - dim - 1))

    loudness = one(*shards[0])
    for cut in shards[1:]:
        loudness = loudness * one(*cut)
    return loudness


def noise(key, shape, deviation, most, split=(), kind=jnp.bfloat16):
    gain = steps_of(key, shape, split, -0.22, 0.18) if split else 1.0
    values = jax.random.normal(key, shape, jnp.float32) * deviation * gain
    return jnp.minimum(jnp.maximum(values, -most), most).astype(kind)


def heavy_noise(stream_key, dims, deviation, limit, split, heavy, kind=jnp.bfloat16):
    result = deviation * jax.random.normal(stream_key, dims, jnp.float32)
    if split:
        result = result * steps_of(stream_key, dims, split, -0.22, 0.18)
    return jnp.clip(spiked(result, jax.random.fold_in(stream_key, 3), *heavy), -limit, limit).astype(kind)


def setup_inputs(seed: int = 0) -> dict:
    splits = jax.random.split(jax.random.key(seed), 9)
    prompt_hidden = heavy_noise(splits[0], (N_DP * PROMPT_DEV, D), 1.0, 6.0, ((0, 32),), (0, 1, 32, 2.75))
    kv_weight = noise(splits[1], (D, 2, KVH * HD), D ** -0.5, 0.078125, ((2, 4),))
    queries = draw_queries(jax.random.fold_in(splits[8], 71), 0)
    out_grad = noise(splits[3], (N_DP * SLOTS, RESP, H * HD), 1.0, 6.0, ((0, 32), (2, 4)))
    own_kv = draw_own_kv(jax.random.fold_in(splits[8], 71), 0)
    pack_counts = draw_pack_counts(jax.random.fold_in(splits[8], 71), 0)
    slot_groups = draw_slot_groups(jax.random.fold_in(splits[8], 71), 0)
    block_group = draw_block_group(jax.random.fold_in(splits[8], 71), 0)
    return dict(prompt_hidden=prompt_hidden, kv_weight=kv_weight, queries=queries, out_grad=out_grad, own_kv=own_kv, pack_counts=pack_counts, slot_groups=slot_groups, block_group=block_group)


def attend(queries, grads, own, prefix, score_scale):
    plen = prefix.shape[0]
    keys = jnp.concatenate([prefix[:, 0], own[:, 0]], 0).astype(jnp.float32)
    values = jnp.concatenate([prefix[:, 1], own[:, 1]], 0).astype(jnp.float32)
    q_full = queries.astype(jnp.float32)
    g_full = grads.astype(jnp.float32)
    scores = jnp.einsum('rkgd,lkd->kgrl', q_full, keys) * score_scale
    query_pos = jnp.arange(queries.shape[0], dtype=jnp.int32)
    key_pos = jnp.arange(keys.shape[0], dtype=jnp.int32)
    visible = (key_pos[None, :] < plen) | (key_pos[None, :] - plen <= query_pos[:, None])
    scores = jnp.where(visible, scores, -1e+30)
    row_max = lax.optimization_barrier(jnp.max(scores, axis=-1, keepdims=True))
    expd = jnp.exp(scores - row_max)
    prob = expd / lax.optimization_barrier(jnp.sum(expd, axis=-1, keepdims=True))
    prob_b = prob.astype(jnp.bfloat16).astype(jnp.float32)
    attended = jnp.einsum('kgrl,lkd->rkgd', prob_b, values)
    delta = jnp.transpose(lax.optimization_barrier(jnp.sum(g_full * attended, axis=-1)), (1, 2, 0))
    dprob = jnp.einsum('rkgd,lkd->kgrl', g_full, values)
    dscore = (prob * (dprob - delta[..., None])).astype(jnp.bfloat16).astype(jnp.float32)
    query_grad = jnp.einsum('kgrl,lkd->rkgd', dscore, keys) * score_scale
    key_grads = jnp.einsum('kgrl,rkgd->lkd', dscore, q_full) * score_scale
    value_grads = jnp.einsum('kgrl,rkgd->lkd', prob_b, g_full)
    both = jnp.stack([key_grads, value_grads], 1)
    return (attended.astype(jnp.bfloat16), query_grad.astype(jnp.bfloat16), both[plen:].astype(jnp.bfloat16), both[:plen])

def reference(prompt_hidden, kv_weight, queries, out_grad, own_kv, pack_counts, slot_groups, block_group):
    kv_width = KVH * HD
    repeats = H // KVH
    score_scale = 1.0 / math.sqrt(HD)
    prompt_kv = jnp.dot(prompt_hidden, kv_weight.reshape(D, 2 * kv_width), preferred_element_type=jnp.float32).astype(jnp.bfloat16)
    blocks_kv = prompt_kv.reshape(N_DP, PROMPT_DEV, 2, KVH, HD)
    group_blocks = jnp.argsort(block_group, stable=True).astype(jnp.int32).reshape(GROUPS, BLOCKS)
    used = (jnp.arange(SLOTS, dtype=jnp.int32)[None, :] < pack_counts[:, None]).reshape(-1)
    order = jnp.argsort(1 - used.astype(jnp.int32), stable=True)[:GROUPS * GROUP].astype(jnp.int32)
    groups_flat = slot_groups.reshape(-1)

    def step(accum, index):
        q_slot = queries[index].reshape(RESP, KVH, repeats, HD)
        g_slot = out_grad[index].reshape(RESP, KVH, repeats, HD)
        own_slot = own_kv[index].reshape(RESP, 2, KVH, HD)
        chosen = group_blocks[groups_flat[index]]
        prefix = blocks_kv[chosen].reshape(PROMPT, 2, KVH, HD)
        attended, query_grad, own_grad, prefix_grad = attend(q_slot, g_slot, own_slot, prefix, score_scale)
        accum = accum.at[chosen].add(prefix_grad.reshape(BLOCKS, PROMPT_DEV, 2, KVH, HD))
        return (accum, (attended.reshape(RESP, H * HD), query_grad.reshape(RESP, H * HD), own_grad.reshape(RESP, 2, kv_width)))
    start_acc = jnp.zeros((N_DP, PROMPT_DEV, 2, KVH, HD), jnp.float32)
    accum, (attended_all, qgrad_all, owngrad_all) = lax.scan(step, start_acc, order)
    attn_out = jnp.zeros(queries.shape, jnp.bfloat16).at[order].set(attended_all)
    query_grad = jnp.zeros(queries.shape, jnp.bfloat16).at[order].set(qgrad_all)
    own_kv_grad = jnp.zeros(own_kv.shape, jnp.bfloat16).at[order].set(owngrad_all)
    block_b = accum.astype(jnp.bfloat16).reshape(N_DP, PROMPT_DEV, 2 * kv_width)
    hidden_blocks = prompt_hidden.reshape(N_DP, PROMPT_DEV, D)

    def weight_step(total, pair):
        hidden_rows, grad_rows = pair
        term = jnp.dot(hidden_rows.T, grad_rows, preferred_element_type=jnp.float32).astype(jnp.bfloat16)
        term = lax.optimization_barrier(term)
        return (total + term.astype(jnp.float32), None)
    weight_grad, _ = lax.scan(weight_step, jnp.zeros((D, 2 * kv_width), jnp.float32), (hidden_blocks, block_b))
    prompt_grad = jnp.dot(block_b.reshape(N_DP * PROMPT_DEV, 2 * kv_width), kv_weight.reshape(D, 2 * kv_width).T, preferred_element_type=jnp.float32).astype(jnp.bfloat16)
    return (attn_out, query_grad, own_kv_grad, weight_grad.reshape(D, 2, kv_width), prompt_grad)
```

```python
import functools
import math

import jax
import jax.numpy as jnp
from jax import lax
from jax.experimental import pallas as pl
from jax.experimental.pallas import tpu as pltpu
from jax.sharding import Mesh, PartitionSpec as P

HD = 128
GROUP = 16
GROUPS = 8
BLOCKS = 4
SLOTS = 8
RESP = 128
REPEATS = 5
N_DP = 32
F32 = jnp.float32
BF16 = jnp.bfloat16
SCALE = 1.0 / math.sqrt(HD)
LOG2_SCALE = SCALE * math.log2(math.e)
NT = (((1,), (1,)), ((), ()))
NN = (((1,), (0,)), ((), ()))


def dot(a, b, dims):
    return lax.dot_general(a, b, dims, preferred_element_type=F32)


def attention_kernel(
    chosen_ref, info_ref, q_ref, g_ref, own_k_ref, own_v_ref, near_ref, far_ref, *rest
):
    out_ref, qgrad_ref, own_kg_ref, own_vg_ref, keep_ref, send_ref, accum = rest[-7:]
    slot = pl.program_id(0)
    used = slot < info_ref[0]
    core = info_ref[1]
    prefix_rows = BLOCKS * RESP

    @pl.when(slot == 0)
    def _():
        accum[...] = jnp.zeros_like(accum)

    @pl.when(jnp.logical_not(used))
    def _():
        out_ref[...] = jnp.zeros_like(out_ref)
        qgrad_ref[...] = jnp.zeros_like(qgrad_ref)
        own_kg_ref[...] = jnp.zeros_like(own_kg_ref)
        own_vg_ref[...] = jnp.zeros_like(own_vg_ref)

    @pl.when(used)
    def _():
        ids = [chosen_ref[slot, j] for j in range(BLOCKS)]
        near = jnp.concatenate([near_ref[i] for i in ids], 0)
        far = jnp.concatenate([far_ref[i] for i in ids], 0)
        first = core == 0
        keys = jnp.concatenate([jnp.where(first, near, far), own_k_ref[0]], 0)
        values = jnp.concatenate([jnp.where(first, far, near), own_v_ref[0]], 0)
        q_wide, g_wide = q_ref[0], g_ref[0]
        heads = [slice(r * HD, (r + 1) * HD) for r in range(REPEATS)]
        queries = jnp.concatenate([q_wide[:, h] for h in heads], 0)
        grads = jnp.concatenate([g_wide[:, h] for h in heads], 0)
        key_pos = lax.broadcasted_iota(jnp.int32, (RESP, RESP), 0)
        query_pos = lax.broadcasted_iota(jnp.int32, (RESP, RESP), 1)
        visible = jnp.concatenate([key_pos <= query_pos] * REPEATS, 1)
        scores = dot(keys, queries, NT)
        scores = jnp.concatenate(
            [scores[:prefix_rows], jnp.where(visible, scores[prefix_rows:], -1e30)], 0
        )
        top = jnp.max(scores, 0, keepdims=True)
        expd = jnp.exp2((scores - top) * LOG2_SCALE)
        prob = expd * (1.0 / jnp.sum(expd, 0, keepdims=True))
        prob_b = prob.astype(BF16)
        dprob = dot(values, grads, NT)
        delta = jnp.sum(prob_b.astype(F32) * dprob, 0, keepdims=True)
        dscore = (prob * (dprob - delta)).astype(BF16)
        attended = dot(values.T, prob_b, NN)
        query_grad = dot(keys.T, dscore, NN)
        for r, h in enumerate(heads):
            out_ref[0, :, h] = attended[:, h].T.astype(BF16)
            qgrad_ref[0, :, h] = (query_grad[:, h].T * SCALE).astype(BF16)
        value_grads = dot(prob_b, grads, NN)
        key_grads = dot(dscore, queries, NN) * SCALE
        for j, i in enumerate(ids):
            rows = slice(j * RESP, (j + 1) * RESP)
            accum[i, :, :HD] += key_grads[rows]
            accum[i, :, HD:] += value_grads[rows]
        own_kg_ref[0] = key_grads[prefix_rows:].astype(BF16)
        own_vg_ref[0] = value_grads[prefix_rows:].astype(BF16)

    @pl.when(slot == SLOTS - 1)
    def _():
        for chip in range(N_DP // 2):
            keep_ref[chip] = accum[2 * chip + core].astype(BF16)
            send_ref[chip] = accum[2 * chip + 1 - core].astype(BF16)


def attention(head, chosen, info, queries, out_grad, own, near, far, written):
    wide = pl.BlockSpec((1, RESP, REPEATS * HD), lambda s, *_: (s, 0, head))
    whole = pl.BlockSpec((N_DP, RESP, HD), lambda s, *_: (0, 0, 0))
    narrow = pl.BlockSpec((1, RESP, HD), lambda s, *_: (s, 0, 0))
    shared = pl.BlockSpec((N_DP // 2, RESP, 2 * HD), lambda s, *_: (0, 0, 0))
    in_specs = [
        wide,
        wide,
        pl.BlockSpec((1, RESP, HD), lambda s, *_: (s, 0, head)),
        pl.BlockSpec((1, RESP, HD), lambda s, *_: (s, 0, 2 + head)),
        whole,
        whole,
    ] + [pl.BlockSpec(memory_space=pl.ANY)] * len(written)
    return pl.pallas_call(
        attention_kernel,
        grid_spec=pltpu.PrefetchScalarGridSpec(
            num_scalar_prefetch=2,
            grid=(SLOTS,),
            in_specs=in_specs,
            out_specs=[wide, wide, narrow, narrow, shared, shared],
            scratch_shapes=[pltpu.VMEM((N_DP, RESP, 2 * HD), F32)],
        ),
        out_shape=[
            jax.ShapeDtypeStruct(queries.shape, BF16),
            jax.ShapeDtypeStruct(queries.shape, BF16),
            jax.ShapeDtypeStruct((SLOTS, RESP, HD), BF16),
            jax.ShapeDtypeStruct((SLOTS, RESP, HD), BF16),
            jax.ShapeDtypeStruct((N_DP // 2, RESP, 2 * HD), BF16),
            jax.ShapeDtypeStruct((N_DP // 2, RESP, 2 * HD), BF16),
        ],
        input_output_aliases={8 + i: i for i in range(len(written))},
        cost_estimate=pl.CostEstimate(
            flops=6 * 2 * SLOTS * REPEATS * RESP * (BLOCKS + 1) * RESP * HD,
            bytes_accessed=16 * 2**20,
            transcendentals=SLOTS * REPEATS * RESP * (BLOCKS + 1) * RESP,
        ),
        compiler_params=pltpu.CompilerParams(vmem_limit_bytes=56 * 2**20),
        name="attention",
    )(chosen, info, queries, out_grad, own, own, near, far, *written)


def swap_cores(array):
    return lax.ppermute(array, "c", [(0, 1), (1, 0)])


def exchange(array, axes):
    return lax.all_to_all(array, axes, 0, 0, tiled=True)


def body(
    prompt_hidden, kv_weight, queries, out_grad, own_kv, pack_counts, slot_groups, block_group
):
    width = prompt_hidden.shape[1]
    core = lax.axis_index("c")
    first = core == 0
    me = lax.axis_index(("y", "z", "c"))
    weight = kv_weight.reshape(width, 4 * HD)
    projected = jnp.dot(prompt_hidden, weight, preferred_element_type=F32).astype(BF16)

    keys, values = projected[:, : 2 * HD], projected[:, 2 * HD :]
    kept = jnp.where(first, keys, values)
    got = swap_cores(jnp.where(first, values, keys))
    chip = jnp.concatenate([jnp.where(first, kept, got), jnp.where(first, got, kept)], 0)

    def gather(head):
        piece = chip[:, head * HD : (head + 1) * HD]
        return exchange(jnp.broadcast_to(piece[None], (16, 2 * RESP, HD)), ("y", "z"))

    halves = [gather(head).reshape(N_DP, RESP, HD) for head in range(2)]

    block = jnp.arange(N_DP, dtype=jnp.int32)
    before = (block_group[None, :] < block_group[:, None]) | (
        (block_group[None, :] == block_group[:, None]) & (block[None, :] < block[:, None])
    )
    rank = jnp.sum(before.astype(jnp.int32), 1)
    order = jnp.sum(jnp.where(rank[None, :] == block[:, None], block[None, :], 0), 1)
    mine = lax.dynamic_index_in_dim(slot_groups, me, 0, keepdims=False)
    place = mine[:, None] * BLOCKS + jnp.arange(BLOCKS, dtype=jnp.int32)[None, :]
    chosen = jnp.sum(
        jnp.where(place[:, :, None] == block[None, None, :], order[None, None, :], 0), 2
    )
    count = lax.dynamic_index_in_dim(pack_counts, me, 0, keepdims=False)
    info = jnp.stack([count, core.astype(jnp.int32)])
    own = own_kv.reshape(SLOTS, RESP, 4 * HD)

    share = width // N_DP
    columns = prompt_hidden.reshape(RESP, 4, 8, share).transpose(2, 0, 1, 3)
    columns = columns.reshape(8, RESP, 4 * share)
    columns, halves[0] = lax.optimization_barrier((columns, halves[0]))
    hidden_y = exchange(columns, ("z", "c")).reshape(8 * RESP, 4 * share)

    written = ()
    own_keys, own_values, keeps, sends = [], [], [], []
    for head in range(2):
        near = halves[head]
        outs, qgrads, own_k, own_v, keep, send = attention(
            head, chosen, info, queries, out_grad, own, near, swap_cores(near), written
        )
        written = (outs, qgrads)
        own_keys.append(own_k)
        own_values.append(own_v)
        keeps.append(keep)
        sends.append(send)
    own_grad = jnp.stack(
        [jnp.concatenate(own_keys, 2), jnp.concatenate(own_values, 2)], 2
    )

    partial = [
        (keep.astype(F32) + swap_cores(send).astype(F32)).astype(BF16)
        for keep, send in zip(keeps, sends)
    ]
    partial = jnp.concatenate(
        [p[:, :, :HD] for p in partial] + [p[:, :, HD:] for p in partial], 2
    )
    block_b = jnp.sum(exchange(partial, ("y", "z")).astype(F32), 0).astype(BF16)

    hidden_term = jnp.einsum(
        "pc,xdc->xpd",
        block_b,
        weight.reshape(4, width // 4, 4 * HD),
        preferred_element_type=F32,
    ).astype(BF16)
    prompt_grad = jnp.sum(exchange(hidden_term, "x").astype(F32), 0).astype(BF16)

    line = exchange(jnp.broadcast_to(block_b[None], (4,) + block_b.shape), "z")
    other = swap_cores(line)
    pair = jnp.stack([jnp.where(first, line, other), jnp.where(first, other, line)], 1)
    term = jnp.einsum(
        "pd,pc->dc",
        hidden_y,
        pair.reshape(8 * RESP, 4 * HD),
        preferred_element_type=F32,
    ).astype(BF16)
    weight_grad = jnp.sum(exchange(term.reshape(4, share, 4 * HD), "y").astype(F32), 0)
    return (outs, qgrads, own_grad, weight_grad.reshape(share, 2, 2 * HD), prompt_grad)


def solution(mesh):
    grid = Mesh(mesh.devices.reshape(4, 4, 2, 4), ("y", "z", "c", "x"))
    dp = ("y", "z", "c")
    return jax.shard_map(
        body,
        mesh=grid,
        in_specs=(
            P(dp, None),
            P(None, None, "x"),
            P(dp, None, "x"),
            P(dp, None, "x"),
            P(dp, None, None, "x"),
            P(),
            P(),
            P(),
        ),
        out_specs=(
            P(dp, None, "x"),
            P(dp, None, "x"),
            P(dp, None, None, "x"),
            P(dp, None, "x"),
            P(dp, "x"),
        ),
        check_vma=False,
    )
```

```python
import functools
import math

import jax
import jax.numpy as jnp
from jax import lax
from jax.experimental import pallas as pl
from jax.experimental.pallas import tpu as pltpu
from jax.sharding import Mesh, PartitionSpec as P

HD = 128
GROUP = 16
GROUPS = 8
BLOCKS = 4
SLOTS = 8
RESP = 128
REPEATS = 5
N_DP = 32
F32 = jnp.float32
BF16 = jnp.bfloat16
SCALE = 1.0 / math.sqrt(HD)
LOG2_SCALE = SCALE * math.log2(math.e)
NT = (((1,), (1,)), ((), ()))
NN = (((1,), (0,)), ((), ()))


def dot(a, b, dims):
    return lax.dot_general(a, b, dims, preferred_element_type=F32)


def attention_kernel(
    pack_counts, slot_groups, block_group, queries_hbm, grads_hbm, own_hbm, near, far,
    out_hbm, qgrad_hbm, own_grad_hbm, keep_hbm, send_hbm,
    queries, grads, out, qgrad, own, own_grad, keep, send, accum,
    expd_0, expd_1, inverse_0, inverse_1, order, filled, sems,
):
    core = lax.axis_index("c")
    me = (lax.axis_index("y") * 4 + lax.axis_index("z")) * 2 + core
    count = pack_counts[me]
    first = core == 0
    prefix_rows = BLOCKS * RESP
    states = ((expd_0, inverse_0), (expd_1, inverse_1))

    def loads(slot):
        return (
            pltpu.make_async_copy(queries_hbm.at[slot], queries.at[slot], sems.at[2, slot]),
            pltpu.make_async_copy(grads_hbm.at[slot], grads.at[slot], sems.at[3, slot]),
            pltpu.make_async_copy(own_hbm.at[slot], own.at[slot], sems.at[4, slot]),
        )

    def stores(slot):
        return (
            pltpu.make_async_copy(out.at[slot], out_hbm.at[slot], sems.at[0, slot]),
            pltpu.make_async_copy(qgrad.at[slot], qgrad_hbm.at[slot], sems.at[1, slot]),
            pltpu.make_async_copy(own_grad.at[slot], own_grad_hbm.at[slot], sems.at[5, slot]),
        )

    @pl.loop(0, jnp.minimum(count, 2))
    def _(slot):
        for copy in loads(slot):
            copy.start()

    for group in range(GROUPS):
        filled[group] = 0

    @pl.loop(0, N_DP)
    def _(block):
        group = block_group[block]
        order[group * BLOCKS + filled[group]] = block
        filled[group] = filled[group] + 1

    accum[...] = jnp.zeros_like(accum)

    @pl.loop(count, SLOTS)
    def _(slot):
        out[slot] = jnp.zeros(out.shape[1:], BF16)
        qgrad[slot] = jnp.zeros(qgrad.shape[1:], BF16)
        own_grad[slot] = jnp.zeros(own_grad.shape[1:], BF16)
        for copy in stores(slot):
            copy.start()

    key_pos = lax.broadcasted_iota(jnp.int32, (RESP, RESP), 0)
    query_pos = lax.broadcasted_iota(jnp.int32, (RESP, RESP), 1)

    def columns(part):
        return slice(part * HD, (part + 1) * HD)

    def blocks_of(slot):
        group = slot_groups[slot, me]
        return [order[group * BLOCKS + j] for j in range(BLOCKS)]

    def keys_values(slot, head):
        ids, cols = blocks_of(slot), columns(head)
        ours = jnp.concatenate([near[i, :, cols] for i in ids], 0)
        theirs = jnp.concatenate([far[i, :, cols] for i in ids], 0)
        keys, values = jnp.where(first, ours, theirs), jnp.where(first, theirs, ours)
        return (
            jnp.concatenate([keys, own[slot, :, cols]], 0),
            jnp.concatenate([values, own[slot, :, columns(2 + head)]], 0),
        )

    def query_rows(slot, head):
        return jnp.concatenate(
            [queries[slot, :, columns(head * REPEATS + r)] for r in range(REPEATS)], 0
        )

    def softmax(slot, head):
        expd_ref, inverse_ref = states[head]
        keys, _ = keys_values(slot, head)
        scores = dot(keys, query_rows(slot, head), NT)
        yield
        visible = jnp.concatenate([key_pos <= query_pos] * REPEATS, 1)
        scores = jnp.concatenate(
            [scores[:prefix_rows], jnp.where(visible, scores[prefix_rows:], -1e30)], 0
        )
        top = jnp.max(scores, 0, keepdims=True)
        yield
        expd = jnp.exp2((scores - top) * LOG2_SCALE)
        expd_ref[...] = expd.astype(BF16)
        yield
        inverse_ref[...] = 1.0 / jnp.sum(expd, 0, keepdims=True)

    def gradients(slot, head):
        expd_ref, inverse_ref = states[head]
        keys, values = keys_values(slot, head)
        expd, inverse = expd_ref[...], inverse_ref[...]
        attended = dot(values.T, expd, NN) * inverse
        scaled = jnp.concatenate(
            [grads[slot, :, columns(head * REPEATS + r)].T for r in range(REPEATS)], 1
        )
        scaled = (scaled.astype(F32) * inverse).astype(BF16)
        yield
        delta = jnp.sum(scaled.astype(F32) * attended, 0, keepdims=True)
        dprob = dot(values, scaled, NN)
        yield
        dscore = expd * (dprob - delta).astype(BF16)
        value_grads = dot(expd, scaled, NT)
        yield
        query_grad = dot(keys.T, dscore, NN) * SCALE
        key_grads = dot(dscore, query_rows(slot, head), NN) * SCALE
        yield
        for r in range(REPEATS):
            rows = slice(r * RESP, (r + 1) * RESP)
            cols = columns(head * REPEATS + r)
            out[slot, :, cols] = attended[:, rows].T.astype(BF16)
            qgrad[slot, :, cols] = query_grad[:, rows].T.astype(BF16)
        for j, i in enumerate(blocks_of(slot)):
            rows = slice(j * RESP, (j + 1) * RESP)
            accum[i, :, columns(head)] += key_grads[rows]
            accum[i, :, columns(2 + head)] += value_grads[rows]
        own_grad[slot, :, columns(head)] = key_grads[prefix_rows:].astype(BF16)
        own_grad[slot, :, columns(2 + head)] = value_grads[prefix_rows:].astype(BF16)

    def together(*parts):
        parts = list(parts)
        while parts:
            parts = [part for part in parts if next(part, part) is None]

    @pl.when(count > 0)
    def _():
        for copy in loads(0):
            copy.wait()
        together(softmax(0, 0))

    @pl.loop(0, count)
    def _(slot):
        later = jnp.minimum(slot + 1, count - 1)

        @pl.when(slot + 2 < count)
        def _():
            for copy in loads(slot + 2):
                copy.start()

        @pl.when(later > slot)
        def _():
            for copy in loads(later):
                copy.wait()

        together(gradients(slot, 0), softmax(slot, 1))
        together(gradients(slot, 1), softmax(later, 0))
        for copy in stores(slot):
            copy.start()

    halves = []
    for place, (half, half_hbm, mine) in enumerate(
        ((send, send_hbm, 1 - core), (keep, keep_hbm, core))
    ):
        for part in range(4):
            chips = pl.ds(4 * part, 4)
            for chip in range(4 * part, 4 * part + 4):
                half[chip] = accum[2 * chip + mine].astype(BF16)
            copy = pltpu.make_async_copy(
                half.at[chips], half_hbm.at[chips], sems.at[6 + place, part]
            )
            copy.start()
            halves.append(copy)

    @pl.loop(0, SLOTS)
    def _(slot):
        for copy in stores(slot):
            copy.wait()

    for copy in halves:
        copy.wait()


def after_kernel(*refs):
    del refs


def after(array, tokens, space):
    anywhere = pl.BlockSpec(memory_space=pl.ANY)
    spec = pl.BlockSpec(memory_space=space)
    return pl.pallas_call(
        after_kernel,
        in_specs=[spec] + [anywhere] * len(tokens),
        out_specs=spec,
        out_shape=space(array.shape, array.dtype),
        input_output_aliases={0: 0},
        compiler_params=pltpu.CompilerParams(vmem_limit_bytes=2**20),
        name="after",
    )(
        pltpu.with_memory_space_constraint(array, space),
        *tokens,
    )


def columns_kernel(hidden, columns):
    share = hidden.shape[1] // N_DP
    for part in range(8):
        for y in range(4):
            start = (8 * y + part) * share
            columns[part, y * share : (y + 1) * share] = hidden[:, start : start + share].T


def columns_of(hidden):
    rows, width = hidden.shape
    return pl.pallas_call(
        columns_kernel,
        out_shape=jax.ShapeDtypeStruct((8, width // 8, rows), BF16),
        compiler_params=pltpu.CompilerParams(vmem_limit_bytes=8 * 2**20),
        name="columns",
    )(hidden)


def total_kernel(parts, total, copies):
    summed = parts[0].astype(F32)
    for i in range(1, parts.shape[0]):
        summed = summed + parts[i].astype(F32)
    summed = summed.astype(BF16)
    total[...] = summed
    for i in range(copies.shape[0]):
        copies[i] = summed


def total_of(parts):
    shape = parts.shape[1:]
    return pl.pallas_call(
        total_kernel,
        out_shape=[
            jax.ShapeDtypeStruct(shape, BF16),
            jax.ShapeDtypeStruct((4,) + shape, BF16),
        ],
        compiler_params=pltpu.CompilerParams(vmem_limit_bytes=8 * 2**20),
        name="total",
    )(parts)


def term_kernel(hidden, line, other, *refs):
    *parts, terms = refs
    first = lax.axis_index("c") == 0
    total = None
    for z in range(4):
        ours, theirs = line[z], other[z]
        pair = jnp.concatenate(
            [jnp.where(first, ours, theirs), jnp.where(first, theirs, ours)], 0
        )
        both = jnp.concatenate([hidden[2 * z], hidden[2 * z + 1]], 1)
        part = dot(both, pair, NN)
        total = part if total is None else total + part
    terms[...] = total
    share = parts[0].shape[0]
    here = lax.axis_index("y")
    for step, part in enumerate(parts):
        start = pl.multiple_of(lax.rem(here + step, 4) * share, share)
        part[...] = terms[pl.ds(start, share)].astype(BF16)


def term_of(hidden, line, other):
    width, columns = hidden.shape[1], line.shape[2]
    return pl.pallas_call(
        term_kernel,
        out_shape=[jax.ShapeDtypeStruct((width // 4, columns), BF16)] * 4,
        scratch_shapes=[pltpu.VMEM((width, columns), F32)],
        compiler_params=pltpu.CompilerParams(vmem_limit_bytes=12 * 2**20),
        name="term",
    )(hidden, line, other)


def prompt_kernel(block, weight_hbm, terms, weight, sems):
    rows = terms.shape[2]
    copies = [
        pltpu.make_async_copy(
            weight_hbm.at[:, pl.ds(x * rows, rows)], weight.at[x], sems.at[x]
        )
        for x in range(4)
    ]
    for copy in copies:
        copy.start()
    for x, copy in enumerate(copies):
        copy.wait()
        terms[x] = (
            dot(block[:, : 2 * HD], weight[x, 0], NT)
            + dot(block[:, 2 * HD :], weight[x, 1], NT)
        ).astype(BF16)


def prompt_terms(block, weight):
    shape = (4, block.shape[0], weight.shape[1] // 4)
    return pl.pallas_call(
        prompt_kernel,
        out_shape=jax.ShapeDtypeStruct(shape, BF16),
        in_specs=[
            pl.BlockSpec(memory_space=pltpu.VMEM),
            pl.BlockSpec(memory_space=pl.ANY),
        ],
        scratch_shapes=[
            pltpu.VMEM((4, 2, shape[2], 2 * HD), BF16),
            pltpu.SemaphoreType.DMA((4,)),
        ],
        cost_estimate=pl.CostEstimate(
            flops=8 * shape[1] * shape[2] * 4 * HD, bytes_accessed=2**22, transcendentals=0
        ),
        compiler_params=pltpu.CompilerParams(vmem_limit_bytes=16 * 2**20),
        name="prompt",
    )(block, in_hbm(weight))


def sum_kernel(*refs):
    *parts, result = refs
    total = None
    for part in parts:
        values = [part[i] for i in range(part.shape[0])] if part.ndim == 3 else [part[...]]
        for value in values:
            value = value.astype(F32)
            total = value if total is None else total + value
    result[...] = total.astype(result.dtype)


def sum_of(parts, dtype):
    return pl.pallas_call(
        sum_kernel,
        out_shape=jax.ShapeDtypeStruct(parts[0].shape[-2:], dtype),
        compiler_params=pltpu.CompilerParams(vmem_limit_bytes=8 * 2**20),
        name="sum",
    )(*parts)


def attention(pack_counts, slot_groups, block_group, queries, out_grad, own, near, far):
    vmem = pl.BlockSpec(memory_space=pltpu.VMEM)
    smem = pl.BlockSpec(memory_space=pltpu.SMEM)
    anywhere = pl.BlockSpec(memory_space=pl.ANY)
    rows = BLOCKS * RESP + RESP
    shared = (N_DP // 2, RESP, 4 * HD)
    outer = [in_hbm(array) for array in (queries, out_grad, own)]
    inner = [pltpu.with_memory_space_constraint(array, pltpu.VMEM) for array in (near, far)]
    return pl.pallas_call(
        attention_kernel,
        in_specs=[smem] * 3 + [anywhere] * 3 + [vmem] * 2,
        out_specs=[anywhere] * 5,
        out_shape=[
            pltpu.HBM(queries.shape, BF16),
            pltpu.HBM(queries.shape, BF16),
            pltpu.HBM(own.shape, BF16),
            pltpu.HBM(shared, BF16),
            pltpu.HBM(shared, BF16),
        ],
        scratch_shapes=[pltpu.VMEM(queries.shape, BF16)] * 4
        + [pltpu.VMEM(own.shape, BF16)] * 2
        + [pltpu.VMEM(shared, BF16)] * 2
        + [
            pltpu.VMEM((N_DP, RESP, 4 * HD), F32),
            pltpu.VMEM((rows, REPEATS * RESP), BF16),
            pltpu.VMEM((rows, REPEATS * RESP), BF16),
            pltpu.VMEM((1, REPEATS * RESP), F32),
            pltpu.VMEM((1, REPEATS * RESP), F32),
            pltpu.SMEM((N_DP,), jnp.int32),
            pltpu.SMEM((GROUPS,), jnp.int32),
            pltpu.SemaphoreType.DMA((8, SLOTS)),
        ],
        cost_estimate=pl.CostEstimate(
            flops=6 * 2 * 2 * SLOTS * REPEATS * RESP * rows * HD,
            bytes_accessed=16 * 2**20,
            transcendentals=2 * SLOTS * REPEATS * RESP * rows,
        ),
        compiler_params=pltpu.CompilerParams(vmem_limit_bytes=40 * 2**20),
        name="attention",
    )(pack_counts, slot_groups.T, block_group, *outer, *inner)


def in_hbm(array):
    return pltpu.with_memory_space_constraint(array, pltpu.HBM)


def swap_cores(array):
    return lax.ppermute(array, "c", [(0, 1), (1, 0)])


def exchange(array, axes):
    return lax.all_to_all(array, axes, 0, 0, tiled=True)


def body(
    prompt_hidden, kv_weight, queries, out_grad, own_kv, pack_counts, slot_groups, block_group
):
    width = prompt_hidden.shape[1]
    core = lax.axis_index("c")
    first = core == 0

    projected = jnp.einsum(
        "pd,dkc->pkc", prompt_hidden, kv_weight, preferred_element_type=F32
    ).astype(BF16)

    keys, values = projected[:, 0], projected[:, 1]
    kept = jnp.where(first, keys, values)
    got = swap_cores(jnp.where(first, values, keys))
    piece = jnp.concatenate([jnp.where(first, kept, got), jnp.where(first, got, kept)], 0)
    piece = jnp.broadcast_to(piece[None], (16, 2 * RESP, 2 * HD))
    near = exchange(piece, ("y", "z")).reshape(N_DP, RESP, 2 * HD)

    own = own_kv.reshape(SLOTS, RESP, 4 * HD)
    columns = columns_of(prompt_hidden)
    relaid = kv_weight.transpose(1, 0, 2)
    near = after(near, (in_hbm(own), in_hbm(columns), in_hbm(relaid)), pltpu.VMEM)
    hidden_y = exchange(columns, ("z", "c"))

    outs, qgrads, own_grad, keep, send = attention(
        pack_counts, slot_groups, block_group, queries, out_grad, own, near, swap_cores(near)
    )
    send = after(send, (hidden_y,), pltpu.HBM)
    partial = (keep.astype(F32) + swap_cores(send).astype(F32)).astype(BF16)
    own_grad = own_grad.reshape(SLOTS, RESP, 2, 2 * HD)
    block_b, line = total_of(exchange(partial, ("y", "z")))
    block_b, own_grad = lax.optimization_barrier((block_b, own_grad))

    terms = prompt_terms(block_b, relaid)
    prompt_grad = sum_of([exchange(terms, "x")], BF16)

    line = after(exchange(line, "z"), (terms,), pltpu.VMEM)
    shares = term_of(hidden_y, line, swap_cores(line))
    moved = [
        lax.ppermute(shares[step], "y", [(i, (i + step) % 4) for i in range(4)])
        for step in (2, 1, 3)
    ]
    weight_grad = sum_of([shares[0], *moved], F32)
    weight_grad = weight_grad.reshape(width // N_DP, 2, 2 * HD)
    return (outs, qgrads, own_grad, weight_grad, prompt_grad)


def solution(mesh):
    grid = Mesh(mesh.devices.reshape(4, 4, 2, 4), ("y", "z", "c", "x"))
    dp = ("y", "z", "c")
    return jax.shard_map(
        body,
        mesh=grid,
        in_specs=(
            P(dp, None),
            P(None, None, "x"),
            P(dp, None, "x"),
            P(dp, None, "x"),
            P(dp, None, None, "x"),
            P(),
            P(),
            P(),
        ),
        out_specs=(
            P(dp, None, "x"),
            P(dp, None, "x"),
            P(dp, None, None, "x"),
            P(dp, None, "x"),
            P(dp, "x"),
        ),
        check_vma=False,
    )
```

```python
import functools
import math

import jax
import jax.numpy as jnp
from jax import lax
from jax.experimental import pallas as pl
from jax.experimental.pallas import tpu as pltpu
from jax.sharding import Mesh, PartitionSpec as P

HD = 128
GROUP = 16
GROUPS = 8
BLOCKS = 4
SLOTS = 8
RESP = 128
REPEATS = 5
N_DP = 32
F32 = jnp.float32
BF16 = jnp.bfloat16
SCALE = 1.0 / math.sqrt(HD)
LOG2_SCALE = SCALE * math.log2(math.e)
NT = (((1,), (1,)), ((), ()))
NN = (((1,), (0,)), ((), ()))


def dot(a, b, dims):
    return lax.dot_general(a, b, dims, preferred_element_type=F32)


def attention_kernel(
    pack_counts, slot_groups, block_group, queries_hbm, grads_hbm, own_hbm, near, far,
    out_hbm, qgrad_hbm, own_grad_hbm, keep_hbm, send_hbm,
    queries, grads, out, qgrad, own, own_grad, keep, send, accum,
    expd_0, expd_1, inverse_0, inverse_1, order, filled, sems,
):
    core = lax.axis_index("c")
    me = (lax.axis_index("y") * 4 + lax.axis_index("z")) * 2 + core
    count = pack_counts[me]
    first = core == 0
    prefix_rows = BLOCKS * RESP
    states = ((expd_0, inverse_0), (expd_1, inverse_1))

    def loads(slot):
        return (
            pltpu.make_async_copy(queries_hbm.at[slot], queries.at[slot], sems.at[2, slot]),
            pltpu.make_async_copy(grads_hbm.at[slot], grads.at[slot], sems.at[3, slot]),
            pltpu.make_async_copy(own_hbm.at[slot], own.at[slot], sems.at[4, slot]),
        )

    def stores(slot):
        return (
            pltpu.make_async_copy(out.at[slot], out_hbm.at[slot], sems.at[0, slot]),
            pltpu.make_async_copy(qgrad.at[slot], qgrad_hbm.at[slot], sems.at[1, slot]),
            pltpu.make_async_copy(own_grad.at[slot], own_grad_hbm.at[slot], sems.at[5, slot]),
        )

    @pl.loop(0, jnp.minimum(count, 2))
    def _(slot):
        for copy in loads(slot):
            copy.start()

    for group in range(GROUPS):
        filled[group] = 0

    @pl.loop(0, N_DP)
    def _(block):
        group = block_group[block]
        order[group * BLOCKS + filled[group]] = block
        filled[group] = filled[group] + 1

    accum[...] = jnp.zeros_like(accum)

    @pl.loop(count, SLOTS)
    def _(slot):
        out[slot] = jnp.zeros(out.shape[1:], BF16)
        qgrad[slot] = jnp.zeros(qgrad.shape[1:], BF16)
        own_grad[slot] = jnp.zeros(own_grad.shape[1:], BF16)
        for copy in stores(slot):
            copy.start()

    key_pos = lax.broadcasted_iota(jnp.int32, (RESP, RESP), 0)
    query_pos = lax.broadcasted_iota(jnp.int32, (RESP, RESP), 1)

    def columns(part):
        return slice(part * HD, (part + 1) * HD)

    def blocks_of(slot):
        group = slot_groups[slot, me]
        return [order[group * BLOCKS + j] for j in range(BLOCKS)]

    def keys_values(slot, head):
        ids, cols = blocks_of(slot), columns(head)
        ours = jnp.concatenate([near[i, :, cols] for i in ids], 0)
        theirs = jnp.concatenate([far[i, :, cols] for i in ids], 0)
        keys, values = jnp.where(first, ours, theirs), jnp.where(first, theirs, ours)
        return (
            jnp.concatenate([keys, own[slot, :, cols]], 0),
            jnp.concatenate([values, own[slot, :, columns(2 + head)]], 0),
        )

    def query_rows(slot, head):
        return jnp.concatenate(
            [queries[slot, :, columns(head * REPEATS + r)] for r in range(REPEATS)], 0
        )

    def softmax(slot, head):
        expd_ref, inverse_ref = states[head]
        keys, _ = keys_values(slot, head)
        scores = dot(keys, query_rows(slot, head), NT)
        yield
        visible = jnp.concatenate([key_pos <= query_pos] * REPEATS, 1)
        scores = jnp.concatenate(
            [scores[:prefix_rows], jnp.where(visible, scores[prefix_rows:], -1e30)], 0
        )
        top = jnp.max(scores, 0, keepdims=True)
        yield
        expd = jnp.exp2((scores - top) * LOG2_SCALE)
        expd_ref[...] = expd.astype(BF16)
        yield
        inverse_ref[...] = 1.0 / jnp.sum(expd, 0, keepdims=True)

    def gradients(slot, head):
        expd_ref, inverse_ref = states[head]
        keys, values = keys_values(slot, head)
        expd, inverse = expd_ref[...], inverse_ref[...]
        attended = dot(values.T, expd, NN) * inverse
        scaled = jnp.concatenate(
            [grads[slot, :, columns(head * REPEATS + r)].T for r in range(REPEATS)], 1
        )
        scaled = (scaled.astype(F32) * inverse).astype(BF16)
        yield
        delta = jnp.sum(scaled.astype(F32) * attended, 0, keepdims=True)
        dprob = dot(values, scaled, NN)
        yield
        dscore = expd * (dprob - delta).astype(BF16)
        value_grads = dot(expd, scaled, NT)
        yield
        query_grad = dot(keys.T, dscore, NN) * SCALE
        key_grads = dot(dscore, query_rows(slot, head), NN) * SCALE
        yield
        for r in range(REPEATS):
            rows = slice(r * RESP, (r + 1) * RESP)
            cols = columns(head * REPEATS + r)
            out[slot, :, cols] = attended[:, rows].T.astype(BF16)
            qgrad[slot, :, cols] = query_grad[:, rows].T.astype(BF16)
        for j, i in enumerate(blocks_of(slot)):
            rows = slice(j * RESP, (j + 1) * RESP)
            accum[i, :, columns(head)] += key_grads[rows]
            accum[i, :, columns(2 + head)] += value_grads[rows]
        own_grad[slot, :, columns(head)] = key_grads[prefix_rows:].astype(BF16)
        own_grad[slot, :, columns(2 + head)] = value_grads[prefix_rows:].astype(BF16)

    def together(*parts):
        parts = list(parts)
        while parts:
            parts = [part for part in parts if next(part, part) is None]

    @pl.when(count > 0)
    def _():
        for copy in loads(0):
            copy.wait()
        together(softmax(0, 0))

    @pl.loop(0, count)
    def _(slot):
        later = jnp.minimum(slot + 1, count - 1)

        @pl.when(slot + 2 < count)
        def _():
            for copy in loads(slot + 2):
                copy.start()

        @pl.when(later > slot)
        def _():
            for copy in loads(later):
                copy.wait()

        together(gradients(slot, 0), softmax(slot, 1))
        together(gradients(slot, 1), softmax(later, 0))
        for copy in stores(slot):
            copy.start()

    halves = []
    for place, (half, half_hbm, mine) in enumerate(
        ((send, send_hbm, 1 - core), (keep, keep_hbm, core))
    ):
        for part in range(4):
            chips = pl.ds(4 * part, 4)
            for chip in range(4 * part, 4 * part + 4):
                half[chip] = accum[2 * chip + mine].astype(BF16)
            copy = pltpu.make_async_copy(
                half.at[chips], half_hbm.at[chips], sems.at[6 + place, part]
            )
            copy.start()
            halves.append(copy)

    @pl.loop(0, SLOTS)
    def _(slot):
        for copy in stores(slot):
            copy.wait()

    for copy in halves:
        copy.wait()


def after_kernel(*refs):
    del refs


def after(array, tokens, space):
    anywhere = pl.BlockSpec(memory_space=pl.ANY)
    spec = pl.BlockSpec(memory_space=space)
    return pl.pallas_call(
        after_kernel,
        in_specs=[spec] + [anywhere] * len(tokens),
        out_specs=spec,
        out_shape=space(array.shape, array.dtype),
        input_output_aliases={0: 0},
        compiler_params=pltpu.CompilerParams(vmem_limit_bytes=2**20),
        name="after",
    )(
        pltpu.with_memory_space_constraint(array, space),
        *tokens,
    )


def after_all(arrays, tokens):
    anywhere = pl.BlockSpec(memory_space=pl.ANY)
    return pl.pallas_call(
        after_kernel,
        in_specs=[anywhere] * (len(arrays) + len(tokens)),
        out_specs=[anywhere] * len(arrays),
        out_shape=[jax.ShapeDtypeStruct(array.shape, array.dtype) for array in arrays],
        input_output_aliases={i: i for i in range(len(arrays))},
        compiler_params=pltpu.CompilerParams(vmem_limit_bytes=2**20),
        name="after",
    )(*arrays, *tokens)


def columns_kernel(hidden, columns):
    share = hidden.shape[1] // N_DP
    for part in range(8):
        for y in range(4):
            start = (8 * y + part) * share
            columns[part, y * share : (y + 1) * share] = hidden[:, start : start + share].T


def columns_of(hidden):
    rows, width = hidden.shape
    return pl.pallas_call(
        columns_kernel,
        out_shape=jax.ShapeDtypeStruct((8, width // 8, rows), BF16),
        compiler_params=pltpu.CompilerParams(vmem_limit_bytes=8 * 2**20),
        name="columns",
    )(hidden)


def term_kernel(hidden, *refs):
    lines, others, parts, terms = refs[:4], refs[4:8], refs[8:12], refs[12]
    first = lax.axis_index("c") == 0
    here = lax.axis_index("z")
    total = None
    for step, (line, other) in enumerate(zip(lines, others)):
        z = lax.rem(here + 4 - step, 4)
        ours, theirs = line[...], other[...]
        pair = jnp.concatenate(
            [jnp.where(first, ours, theirs), jnp.where(first, theirs, ours)], 0
        )
        both = jnp.concatenate([hidden[2 * z], hidden[2 * z + 1]], 1)
        part = dot(both, pair, NN)
        total = part if total is None else total + part
    terms[...] = total
    share = parts[0].shape[0]
    here = lax.axis_index("y")
    for step, part in enumerate(parts):
        start = pl.multiple_of(lax.rem(here + step, 4) * share, share)
        part[...] = terms[pl.ds(start, share)].astype(BF16)


def term_of(hidden, lines, others):
    width, columns = hidden.shape[1], lines[0].shape[1]
    return pl.pallas_call(
        term_kernel,
        out_shape=[jax.ShapeDtypeStruct((width // 4, columns), BF16)] * 4,
        scratch_shapes=[pltpu.VMEM((width, columns), F32)],
        cost_estimate=pl.CostEstimate(
            flops=2000000000, bytes_accessed=10000000, transcendentals=0
        ),
        compiler_params=pltpu.CompilerParams(vmem_limit_bytes=12 * 2**20),
        name="term",
    )(hidden, *lines, *others)


def prompt_kernel(block, weight_hbm, *refs):
    *terms, weight, sems = refs
    here = lax.axis_index("x")
    rows = terms[0].shape[1]
    steps = (2, 1, 3, 0)
    copies = []
    for step in steps:
        start = pl.multiple_of(lax.rem(here + step, 4) * rows, rows)
        copies.append(
            pltpu.make_async_copy(
                weight_hbm.at[:, pl.ds(start, rows)], weight.at[step], sems.at[step]
            )
        )
        copies[-1].start()
    for step, copy in zip(steps, copies):
        copy.wait()
        terms[step][...] = (
            dot(block[:, : 2 * HD], weight[step, 0], NT)
            + dot(block[:, 2 * HD :], weight[step, 1], NT)
        ).astype(BF16)


def prompt_terms(block, weight):
    shape = (block.shape[0], weight.shape[1] // 4)
    return pl.pallas_call(
        prompt_kernel,
        out_shape=[jax.ShapeDtypeStruct(shape, BF16)] * 4,
        in_specs=[
            pl.BlockSpec(memory_space=pltpu.VMEM),
            pl.BlockSpec(memory_space=pl.ANY),
        ],
        scratch_shapes=[
            pltpu.VMEM((4, 2, shape[1], 2 * HD), BF16),
            pltpu.SemaphoreType.DMA((4,)),
        ],
        cost_estimate=pl.CostEstimate(
            flops=8 * shape[0] * shape[1] * 4 * HD, bytes_accessed=2**22, transcendentals=0
        ),
        compiler_params=pltpu.CompilerParams(vmem_limit_bytes=16 * 2**20),
        name="prompt",
    )(block, in_hbm(weight))


def sum_kernel(*refs):
    *parts, result = refs
    total = None
    for part in parts:
        values = [part[i] for i in range(part.shape[0])] if part.ndim == 3 else [part[...]]
        for value in values:
            value = value.astype(F32)
            total = value if total is None else total + value
    result[...] = total.astype(result.dtype)


def sum_of(parts, dtype):
    return pl.pallas_call(
        sum_kernel,
        out_shape=jax.ShapeDtypeStruct(parts[0].shape[-2:], dtype),
        compiler_params=pltpu.CompilerParams(vmem_limit_bytes=8 * 2**20),
        name="sum",
    )(*parts)


def attention(pack_counts, slot_groups, block_group, queries, out_grad, own, near, far):
    vmem = pl.BlockSpec(memory_space=pltpu.VMEM)
    smem = pl.BlockSpec(memory_space=pltpu.SMEM)
    anywhere = pl.BlockSpec(memory_space=pl.ANY)
    rows = BLOCKS * RESP + RESP
    shared = (N_DP // 2, RESP, 4 * HD)
    outer = [in_hbm(array) for array in (queries, out_grad, own)]
    inner = [pltpu.with_memory_space_constraint(array, pltpu.VMEM) for array in (near, far)]
    return pl.pallas_call(
        attention_kernel,
        in_specs=[smem] * 3 + [anywhere] * 3 + [vmem] * 2,
        out_specs=[anywhere] * 5,
        out_shape=[
            pltpu.HBM(queries.shape, BF16),
            pltpu.HBM(queries.shape, BF16),
            pltpu.HBM(own.shape, BF16),
            pltpu.HBM(shared, BF16),
            pltpu.HBM(shared, BF16),
        ],
        scratch_shapes=[pltpu.VMEM(queries.shape, BF16)] * 4
        + [pltpu.VMEM(own.shape, BF16)] * 2
        + [pltpu.VMEM(shared, BF16)] * 2
        + [
            pltpu.VMEM((N_DP, RESP, 4 * HD), F32),
            pltpu.VMEM((rows, REPEATS * RESP), BF16),
            pltpu.VMEM((rows, REPEATS * RESP), BF16),
            pltpu.VMEM((1, REPEATS * RESP), F32),
            pltpu.VMEM((1, REPEATS * RESP), F32),
            pltpu.SMEM((N_DP,), jnp.int32),
            pltpu.SMEM((GROUPS,), jnp.int32),
            pltpu.SemaphoreType.DMA((8, SLOTS)),
        ],
        cost_estimate=pl.CostEstimate(
            flops=6 * 2 * 2 * SLOTS * REPEATS * RESP * rows * HD,
            bytes_accessed=16 * 2**20,
            transcendentals=2 * SLOTS * REPEATS * RESP * rows,
        ),
        compiler_params=pltpu.CompilerParams(vmem_limit_bytes=40 * 2**20),
        name="attention",
    )(pack_counts, slot_groups.T, block_group, *outer, *inner)


def in_hbm(array):
    return pltpu.with_memory_space_constraint(array, pltpu.HBM)


def swap_cores(array):
    return lax.ppermute(array, "c", [(0, 1), (1, 0)])


def exchange(array, axes):
    return lax.all_to_all(array, axes, 0, 0, tiled=True)


def body(
    prompt_hidden, kv_weight, queries, out_grad, own_kv, pack_counts, slot_groups, block_group
):
    width = prompt_hidden.shape[1]
    core = lax.axis_index("c")
    first = core == 0

    projected = jnp.einsum(
        "pd,dkc->pkc", prompt_hidden, kv_weight, preferred_element_type=F32
    ).astype(BF16)

    keys, values = projected[:, 0], projected[:, 1]
    kept = jnp.where(first, keys, values)
    got = swap_cores(jnp.where(first, values, keys))
    piece = jnp.concatenate([jnp.where(first, kept, got), jnp.where(first, got, kept)], 0)
    piece = jnp.broadcast_to(piece[None], (16, 2 * RESP, 2 * HD))
    near = exchange(piece, ("y", "z")).reshape(N_DP, RESP, 2 * HD)

    own = own_kv.reshape(SLOTS, RESP, 4 * HD)
    columns = columns_of(prompt_hidden)
    relaid = kv_weight.transpose(1, 0, 2)
    near = after(near, (in_hbm(own), in_hbm(columns), in_hbm(relaid)), pltpu.VMEM)
    hidden_y = exchange(columns, ("z", "c"))

    outs, qgrads, own_grad, keep, send = attention(
        pack_counts, slot_groups, block_group, queries, out_grad, own, near, swap_cores(near)
    )
    send = after(send, (hidden_y,), pltpu.HBM)
    partial = (keep.astype(F32) + swap_cores(send).astype(F32)).astype(BF16)
    own_grad = own_grad.reshape(SLOTS, RESP, 2, 2 * HD)
    block_b = sum_of([exchange(partial, ("y", "z"))], BF16)

    def ring(array, axis, step):
        return lax.ppermute(array, axis, [(i, (i + step) % 4) for i in range(4)])

    terms = prompt_terms(block_b, relaid)
    prompt_grad = sum_of([terms[0], *[ring(terms[step], "x", step) for step in (2, 1, 3)]], BF16)

    lines = [block_b] + [ring(block_b, "z", step) for step in (1, 2, 3)]
    shares = term_of(hidden_y, lines, [swap_cores(line) for line in lines])
    moved = [ring(shares[step], "y", step) for step in (2, 1, 3)]
    weight_grad = sum_of([shares[0], *moved], F32)
    weight_grad = weight_grad.reshape(width // N_DP, 2, 2 * HD)
    return (outs, qgrads, own_grad, weight_grad, prompt_grad)


def solution(mesh):
    grid = Mesh(mesh.devices.reshape(4, 4, 2, 4), ("y", "z", "c", "x"))
    dp = ("y", "z", "c")
    return jax.shard_map(
        body,
        mesh=grid,
        in_specs=(
            P(dp, None),
            P(None, None, "x"),
            P(dp, None, "x"),
            P(dp, None, "x"),
            P(dp, None, None, "x"),
            P(),
            P(),
            P(),
        ),
        out_specs=(
            P(dp, None, "x"),
            P(dp, None, "x"),
            P(dp, None, None, "x"),
            P(dp, None, "x"),
            P(dp, "x"),
        ),
        check_vma=False,
    )
```

```python
import functools
import math

import jax
import jax.numpy as jnp
from jax import lax
from jax.experimental import pallas as pl
from jax.experimental.pallas import tpu as pltpu
from jax.sharding import Mesh, PartitionSpec as P

HD = 128
GROUP = 16
GROUPS = 8
BLOCKS = 4
SLOTS = 8
RESP = 128
REPEATS = 5
N_DP = 32
F32 = jnp.float32
BF16 = jnp.bfloat16
SCALE = 1.0 / math.sqrt(HD)
LOG2_SCALE = SCALE * math.log2(math.e)
NT = (((1,), (1,)), ((), ()))
NN = (((1,), (0,)), ((), ()))


def dot(a, b, dims):
    return lax.dot_general(a, b, dims, preferred_element_type=F32)


def attention_kernel(
    pack_counts, slot_groups, block_group, queries_hbm, grads_hbm, own_hbm, near, far,
    out_hbm, qgrad_hbm, own_grad_hbm, send_k_hbm, send_v_hbm, keep_k_hbm, keep_v_hbm,
    queries, grads, out, qgrad, own, own_grad, send_k, send_v, keep_k, keep_v, accum,
    expd_0, expd_1, inverse_0, inverse_1, order, filled, sems,
):
    core = lax.axis_index("c")
    me = (lax.axis_index("y") * 4 + lax.axis_index("z")) * 2 + core
    count = pack_counts[me]
    first = core == 0
    prefix_rows = BLOCKS * RESP
    states = ((expd_0, inverse_0), (expd_1, inverse_1))

    def loads(slot):
        return (
            pltpu.make_async_copy(queries_hbm.at[slot], queries.at[slot], sems.at[2, slot]),
            pltpu.make_async_copy(grads_hbm.at[slot], grads.at[slot], sems.at[3, slot]),
            pltpu.make_async_copy(own_hbm.at[slot], own.at[slot], sems.at[4, slot]),
        )

    def stores(slot):
        return (
            pltpu.make_async_copy(out.at[slot], out_hbm.at[slot], sems.at[0, slot]),
            pltpu.make_async_copy(qgrad.at[slot], qgrad_hbm.at[slot], sems.at[1, slot]),
            pltpu.make_async_copy(own_grad.at[slot], own_grad_hbm.at[slot], sems.at[5, slot]),
        )

    @pl.loop(0, jnp.minimum(count, 2))
    def _(slot):
        for copy in loads(slot):
            copy.start()

    for group in range(GROUPS):
        filled[group] = 0

    @pl.loop(0, N_DP)
    def _(block):
        group = block_group[block]
        order[group * BLOCKS + filled[group]] = block
        filled[group] = filled[group] + 1

    accum[...] = jnp.zeros_like(accum)

    @pl.loop(count, SLOTS)
    def _(slot):
        out[slot] = jnp.zeros(out.shape[1:], BF16)
        qgrad[slot] = jnp.zeros(qgrad.shape[1:], BF16)
        own_grad[slot] = jnp.zeros(own_grad.shape[1:], BF16)
        for copy in stores(slot):
            copy.start()

    key_pos = lax.broadcasted_iota(jnp.int32, (RESP, RESP), 0)
    query_pos = lax.broadcasted_iota(jnp.int32, (RESP, RESP), 1)

    def columns(part):
        return slice(part * HD, (part + 1) * HD)

    def blocks_of(slot):
        group = slot_groups[slot, me]
        return [order[group * BLOCKS + j] for j in range(BLOCKS)]

    def keys_values(slot, head):
        ids, cols = blocks_of(slot), columns(head)
        ours = jnp.concatenate([near[i, :, cols] for i in ids], 0)
        theirs = jnp.concatenate([far[i, :, cols] for i in ids], 0)
        keys, values = jnp.where(first, ours, theirs), jnp.where(first, theirs, ours)
        return (
            jnp.concatenate([keys, own[slot, :, cols]], 0),
            jnp.concatenate([values, own[slot, :, columns(2 + head)]], 0),
        )

    def query_rows(slot, head):
        return jnp.concatenate(
            [queries[slot, :, columns(head * REPEATS + r)] for r in range(REPEATS)], 0
        )

    def softmax(slot, head):
        expd_ref, inverse_ref = states[head]
        keys, _ = keys_values(slot, head)
        scores = dot(keys, query_rows(slot, head), NT)
        yield
        visible = jnp.concatenate([key_pos <= query_pos] * REPEATS, 1)
        scores = jnp.concatenate(
            [scores[:prefix_rows], jnp.where(visible, scores[prefix_rows:], -1e30)], 0
        )
        top = jnp.max(scores, 0, keepdims=True)
        yield
        expd = jnp.exp2((scores - top) * LOG2_SCALE)
        expd_ref[...] = expd.astype(BF16)
        yield
        inverse_ref[...] = 1.0 / jnp.sum(expd, 0, keepdims=True)

    def gradients(slot, head):
        expd_ref, inverse_ref = states[head]
        keys, values = keys_values(slot, head)
        expd, inverse = expd_ref[...], inverse_ref[...]
        attended = dot(values.T, expd, NN) * inverse
        scaled = jnp.concatenate(
            [grads[slot, :, columns(head * REPEATS + r)].T for r in range(REPEATS)], 1
        )
        scaled = (scaled.astype(F32) * inverse).astype(BF16)
        yield
        delta = jnp.sum(scaled.astype(F32) * attended, 0, keepdims=True)
        dprob = dot(values, scaled, NN)
        yield
        dscore = expd * (dprob - delta).astype(BF16)
        value_grads = dot(expd, scaled, NT)
        yield
        query_grad = dot(keys.T, dscore, NN) * SCALE
        key_grads = dot(dscore, query_rows(slot, head), NN) * SCALE
        yield
        for r in range(REPEATS):
            rows = slice(r * RESP, (r + 1) * RESP)
            cols = columns(head * REPEATS + r)
            out[slot, :, cols] = attended[:, rows].T.astype(BF16)
            qgrad[slot, :, cols] = query_grad[:, rows].T.astype(BF16)
        for j, i in enumerate(blocks_of(slot)):
            rows = slice(j * RESP, (j + 1) * RESP)
            accum[i, :, columns(head)] += key_grads[rows]
            accum[i, :, columns(2 + head)] += value_grads[rows]
        own_grad[slot, :, columns(head)] = key_grads[prefix_rows:].astype(BF16)
        own_grad[slot, :, columns(2 + head)] = value_grads[prefix_rows:].astype(BF16)

    def together(*parts):
        parts = list(parts)
        while parts:
            parts = [part for part in parts if next(part, part) is None]

    @pl.when(count > 0)
    def _():
        for copy in loads(0):
            copy.wait()
        together(softmax(0, 0))

    @pl.loop(0, count)
    def _(slot):
        later = jnp.minimum(slot + 1, count - 1)

        @pl.when(slot + 2 < count)
        def _():
            for copy in loads(slot + 2):
                copy.start()

        @pl.when(later > slot)
        def _():
            for copy in loads(later):
                copy.wait()

        together(gradients(slot, 0), softmax(slot, 1))
        together(gradients(slot, 1), softmax(later, 0))
        for copy in stores(slot):
            copy.start()

    halves = []
    for place, (half, half_hbm, mine) in enumerate(
        (
            (send_k, send_k_hbm, 1 - core),
            (send_v, send_v_hbm, 1 - core),
            (keep_k, keep_k_hbm, core),
            (keep_v, keep_v_hbm, core),
        )
    ):
        cols = slice(place % 2 * 2 * HD, (place % 2 + 1) * 2 * HD)
        for part in range(4):
            chips = pl.ds(4 * part, 4)
            for chip in range(4 * part, 4 * part + 4):
                half[chip] = accum[2 * chip + mine, :, cols].astype(BF16)
            copy = pltpu.make_async_copy(
                half.at[chips], half_hbm.at[chips], sems.at[6 + place, part]
            )
            copy.start()
            halves.append(copy)

    @pl.loop(0, SLOTS)
    def _(slot):
        for copy in stores(slot):
            copy.wait()

    for copy in halves:
        copy.wait()


def after_kernel(*refs):
    del refs


def after(array, tokens, space):
    anywhere = pl.BlockSpec(memory_space=pl.ANY)
    spec = pl.BlockSpec(memory_space=space)
    return pl.pallas_call(
        after_kernel,
        in_specs=[spec] + [anywhere] * len(tokens),
        out_specs=spec,
        out_shape=space(array.shape, array.dtype),
        input_output_aliases={0: 0},
        compiler_params=pltpu.CompilerParams(vmem_limit_bytes=2**20),
        name="after",
    )(
        pltpu.with_memory_space_constraint(array, space),
        *tokens,
    )


def after_all(arrays, tokens):
    anywhere = pl.BlockSpec(memory_space=pl.ANY)
    return pl.pallas_call(
        after_kernel,
        in_specs=[anywhere] * (len(arrays) + len(tokens)),
        out_specs=[anywhere] * len(arrays),
        out_shape=[jax.ShapeDtypeStruct(array.shape, array.dtype) for array in arrays],
        input_output_aliases={i: i for i in range(len(arrays))},
        compiler_params=pltpu.CompilerParams(vmem_limit_bytes=2**20),
        name="after",
    )(*arrays, *tokens)


def columns_kernel(hidden, columns):
    share = hidden.shape[1] // N_DP
    for part in range(8):
        for y in range(4):
            start = (8 * y + part) * share
            columns[part, y * share : (y + 1) * share] = hidden[:, start : start + share].T


def columns_of(hidden):
    rows, width = hidden.shape
    return pl.pallas_call(
        columns_kernel,
        out_shape=jax.ShapeDtypeStruct((8, width // 8, rows), BF16),
        compiler_params=pltpu.CompilerParams(vmem_limit_bytes=8 * 2**20),
        name="columns",
    )(hidden)


def split_kernel(axis, keep, got, *parts):
    here = lax.axis_index(axis)
    for step, part in enumerate(parts):
        place = lax.rem(here + step, 4)
        for i in range(4):
            chip = place * 4 + i if axis == "y" else i * 4 + place
            part[i] = (keep[chip].astype(F32) + got[chip].astype(F32)).astype(BF16)


def split_sum(keep, got, axis):
    shape = (4,) + keep.shape[1:]
    return pl.pallas_call(
        functools.partial(split_kernel, axis),
        out_shape=[jax.ShapeDtypeStruct(shape, BF16)] * 4,
        compiler_params=pltpu.CompilerParams(vmem_limit_bytes=12 * 2**20),
        name="split",
    )(keep, got)


def reduce_kernel(axis, *refs):
    here = lax.axis_index(axis)
    for step in range(4):
        place = lax.rem(here + step, 4)
        total = refs[0][place].astype(F32)
        for ref in refs[1:4]:
            total = total + ref[place].astype(F32)
        refs[4 + step][...] = total.astype(BF16)


def reduce_of(parts, axis):
    return pl.pallas_call(
        functools.partial(reduce_kernel, axis),
        out_shape=[jax.ShapeDtypeStruct(parts[0].shape[1:], BF16)] * 4,
        compiler_params=pltpu.CompilerParams(vmem_limit_bytes=8 * 2**20),
        name="reduce",
    )(*parts)


def block_kernel(*refs):
    for half in range(2):
        total = refs[4 * half][...].astype(F32)
        for ref in refs[4 * half + 1 : 4 * half + 4]:
            total = total + ref[...].astype(F32)
        refs[8][:, half * 2 * HD : (half + 1) * 2 * HD] = total.astype(BF16)


def block_of(keys, values):
    return pl.pallas_call(
        block_kernel,
        out_shape=jax.ShapeDtypeStruct((keys[0].shape[0], 4 * HD), BF16),
        compiler_params=pltpu.CompilerParams(vmem_limit_bytes=8 * 2**20),
        name="block",
    )(*keys, *values)


def term_kernel(hidden, *refs):
    lines, others, parts, terms = refs[:4], refs[4:8], refs[8:12], refs[12]
    first = lax.axis_index("c") == 0
    here = lax.axis_index("z")
    total = None
    for step, (line, other) in enumerate(zip(lines, others)):
        z = lax.rem(here + 4 - step, 4)
        ours, theirs = line[...], other[...]
        pair = jnp.concatenate(
            [jnp.where(first, ours, theirs), jnp.where(first, theirs, ours)], 0
        )
        both = jnp.concatenate([hidden[2 * z], hidden[2 * z + 1]], 1)
        part = dot(both, pair, NN)
        total = part if total is None else total + part
    terms[...] = total
    share = parts[0].shape[0]
    here = lax.axis_index("y")
    for step, part in enumerate(parts):
        start = pl.multiple_of(lax.rem(here + step, 4) * share, share)
        part[...] = terms[pl.ds(start, share)].astype(BF16)


def term_of(hidden, lines, others):
    width, columns = hidden.shape[1], lines[0].shape[1]
    return pl.pallas_call(
        term_kernel,
        out_shape=[jax.ShapeDtypeStruct((width // 4, columns), BF16)] * 4,
        scratch_shapes=[pltpu.VMEM((width, columns), F32)],
        cost_estimate=pl.CostEstimate(
            flops=2000000000, bytes_accessed=10000000, transcendentals=0
        ),
        compiler_params=pltpu.CompilerParams(vmem_limit_bytes=12 * 2**20),
        name="term",
    )(hidden, *lines, *others)


def prompt_kernel(block, weight_hbm, *refs):
    *terms, weight, sems = refs
    here = lax.axis_index("x")
    rows = terms[0].shape[1]
    steps = (2, 1, 3, 0)
    copies = []
    for step in steps:
        start = pl.multiple_of(lax.rem(here + step, 4) * rows, rows)
        copies.append(
            pltpu.make_async_copy(
                weight_hbm.at[:, pl.ds(start, rows)], weight.at[step], sems.at[step]
            )
        )
        copies[-1].start()
    for step, copy in zip(steps, copies):
        copy.wait()
        terms[step][...] = (
            dot(block[:, : 2 * HD], weight[step, 0], NT)
            + dot(block[:, 2 * HD :], weight[step, 1], NT)
        ).astype(BF16)


def prompt_terms(block, weight):
    shape = (block.shape[0], weight.shape[1] // 4)
    return pl.pallas_call(
        prompt_kernel,
        out_shape=[jax.ShapeDtypeStruct(shape, BF16)] * 4,
        in_specs=[
            pl.BlockSpec(memory_space=pltpu.VMEM),
            pl.BlockSpec(memory_space=pl.ANY),
        ],
        scratch_shapes=[
            pltpu.VMEM((4, 2, shape[1], 2 * HD), BF16),
            pltpu.SemaphoreType.DMA((4,)),
        ],
        cost_estimate=pl.CostEstimate(
            flops=8 * shape[0] * shape[1] * 4 * HD, bytes_accessed=2**22, transcendentals=0
        ),
        compiler_params=pltpu.CompilerParams(vmem_limit_bytes=16 * 2**20),
        name="prompt",
    )(block, in_hbm(weight))


def sum_kernel(*refs):
    *parts, result = refs
    total = None
    for part in parts:
        values = [part[i] for i in range(part.shape[0])] if part.ndim == 3 else [part[...]]
        for value in values:
            value = value.astype(F32)
            total = value if total is None else total + value
    result[...] = total.astype(result.dtype)


def sum_of(parts, dtype):
    return pl.pallas_call(
        sum_kernel,
        out_shape=jax.ShapeDtypeStruct(parts[0].shape[-2:], dtype),
        compiler_params=pltpu.CompilerParams(vmem_limit_bytes=8 * 2**20),
        name="sum",
    )(*parts)


def attention(pack_counts, slot_groups, block_group, queries, out_grad, own, near, far):
    vmem = pl.BlockSpec(memory_space=pltpu.VMEM)
    smem = pl.BlockSpec(memory_space=pltpu.SMEM)
    anywhere = pl.BlockSpec(memory_space=pl.ANY)
    rows = BLOCKS * RESP + RESP
    shared = (N_DP // 2, RESP, 2 * HD)
    outer = [in_hbm(array) for array in (queries, out_grad, own)]
    inner = [pltpu.with_memory_space_constraint(array, pltpu.VMEM) for array in (near, far)]
    return pl.pallas_call(
        attention_kernel,
        in_specs=[smem] * 3 + [anywhere] * 3 + [vmem] * 2,
        out_specs=[anywhere] * 7,
        out_shape=[
            pltpu.HBM(queries.shape, BF16),
            pltpu.HBM(queries.shape, BF16),
            pltpu.HBM(own.shape, BF16),
            *[pltpu.HBM(shared, BF16) for _ in range(4)],
        ],
        scratch_shapes=[pltpu.VMEM(queries.shape, BF16)] * 4
        + [pltpu.VMEM(own.shape, BF16)] * 2
        + [pltpu.VMEM(shared, BF16)] * 4
        + [
            pltpu.VMEM((N_DP, RESP, 4 * HD), F32),
            pltpu.VMEM((rows, REPEATS * RESP), BF16),
            pltpu.VMEM((rows, REPEATS * RESP), BF16),
            pltpu.VMEM((1, REPEATS * RESP), F32),
            pltpu.VMEM((1, REPEATS * RESP), F32),
            pltpu.SMEM((N_DP,), jnp.int32),
            pltpu.SMEM((GROUPS,), jnp.int32),
            pltpu.SemaphoreType.DMA((10, SLOTS)),
        ],
        cost_estimate=pl.CostEstimate(
            flops=6 * 2 * 2 * SLOTS * REPEATS * RESP * rows * HD,
            bytes_accessed=16 * 2**20,
            transcendentals=2 * SLOTS * REPEATS * RESP * rows,
        ),
        compiler_params=pltpu.CompilerParams(vmem_limit_bytes=40 * 2**20),
        name="attention",
    )(pack_counts, slot_groups.T, block_group, *outer, *inner)


def in_hbm(array):
    return pltpu.with_memory_space_constraint(array, pltpu.HBM)


def swap_cores(array):
    return lax.ppermute(array, "c", [(0, 1), (1, 0)])


def exchange(array, axes):
    return lax.all_to_all(array, axes, 0, 0, tiled=True)


def body(
    prompt_hidden, kv_weight, queries, out_grad, own_kv, pack_counts, slot_groups, block_group
):
    width = prompt_hidden.shape[1]
    core = lax.axis_index("c")
    first = core == 0

    projected = jnp.einsum(
        "pd,dkc->pkc", prompt_hidden, kv_weight, preferred_element_type=F32
    ).astype(BF16)

    keys, values = projected[:, 0], projected[:, 1]
    kept = jnp.where(first, keys, values)
    got = swap_cores(jnp.where(first, values, keys))
    piece = jnp.concatenate([jnp.where(first, kept, got), jnp.where(first, got, kept)], 0)
    piece = jnp.broadcast_to(piece[None], (16, 2 * RESP, 2 * HD))
    near = exchange(piece, ("y", "z")).reshape(N_DP, RESP, 2 * HD)

    own = own_kv.reshape(SLOTS, RESP, 4 * HD)
    columns = columns_of(prompt_hidden)
    relaid = kv_weight.transpose(1, 0, 2)
    near = after(near, (in_hbm(own), in_hbm(columns), in_hbm(relaid)), pltpu.VMEM)
    hidden_y = exchange(columns, ("z", "c"))

    outs, qgrads, own_grad, send_k, send_v, keep_k, keep_v = attention(
        pack_counts, slot_groups, block_group, queries, out_grad, own, near, swap_cores(near)
    )
    own_grad = own_grad.reshape(SLOTS, RESP, 2, 2 * HD)

    def ring(array, axis, step):
        return lax.ppermute(array, axis, [(i, (i + step) % 4) for i in range(4)])

    def deal(parts, axis):
        return [parts[0]] + [ring(parts[step], axis, step) for step in (1, 2, 3)]

    send_k = after(send_k, (hidden_y,), pltpu.HBM)
    keys = deal(split_sum(keep_k, swap_cores(send_k), "y"), "y")
    values = deal(split_sum(keep_v, swap_cores(send_v), "z"), "z")
    keys = deal(reduce_of(keys, "z"), "z")
    values = deal(reduce_of(values, "y"), "y")
    block_b = block_of(keys, values)

    terms = prompt_terms(block_b, relaid)
    prompt_grad = sum_of([terms[0], *[ring(terms[step], "x", step) for step in (2, 1, 3)]], BF16)

    lines = [block_b] + [ring(block_b, "z", step) for step in (1, 2, 3)]
    shares = term_of(hidden_y, lines, [swap_cores(line) for line in lines])
    moved = [ring(shares[step], "y", step) for step in (2, 1, 3)]
    weight_grad = sum_of([shares[0], *moved], F32)
    weight_grad = weight_grad.reshape(width // N_DP, 2, 2 * HD)
    return (outs, qgrads, own_grad, weight_grad, prompt_grad)


def solution(mesh):
    grid = Mesh(mesh.devices.reshape(4, 4, 2, 4), ("y", "z", "c", "x"))
    dp = ("y", "z", "c")
    return jax.shard_map(
        body,
        mesh=grid,
        in_specs=(
            P(dp, None),
            P(None, None, "x"),
            P(dp, None, "x"),
            P(dp, None, "x"),
            P(dp, None, None, "x"),
            P(),
            P(),
            P(),
        ),
        out_specs=(
            P(dp, None, "x"),
            P(dp, None, "x"),
            P(dp, None, None, "x"),
            P(dp, None, "x"),
            P(dp, "x"),
        ),
        check_vma=False,
    )
```

```python
import functools
import math

import jax
import jax.numpy as jnp
from jax import lax
from jax.experimental import pallas as pl
from jax.experimental.pallas import tpu as pltpu
from jax.sharding import Mesh, PartitionSpec as P

HD = 128
GROUP = 16
GROUPS = 8
BLOCKS = 4
SLOTS = 8
RESP = 128
REPEATS = 5
N_DP = 32
F32 = jnp.float32
BF16 = jnp.bfloat16
SCALE = 1.0 / math.sqrt(HD)
LOG2_SCALE = SCALE * math.log2(math.e)
NT = (((1,), (1,)), ((), ()))
NN = (((1,), (0,)), ((), ()))


def dot(a, b, dims):
    return lax.dot_general(a, b, dims, preferred_element_type=F32)


def attention_kernel(
    pack_counts, slot_groups, block_group, queries_hbm, grads_hbm, own_hbm, near, far,
    out_hbm, qgrad_hbm, own_grad_hbm, send_k_hbm, send_v_hbm, keep_k_hbm, keep_v_hbm,
    queries, grads, out, qgrad, own, own_grad, send_k, send_v, keep_k, keep_v, accum,
    expd_0, expd_1, inverse_0, inverse_1, order, filled, sems,
):
    core = lax.axis_index("c")
    me = (lax.axis_index("y") * 4 + lax.axis_index("z")) * 2 + core
    count = pack_counts[me]
    first = core == 0
    prefix_rows = BLOCKS * RESP
    states = ((expd_0, inverse_0), (expd_1, inverse_1))

    def loads(slot):
        return (
            pltpu.make_async_copy(queries_hbm.at[slot], queries.at[slot], sems.at[2, slot]),
            pltpu.make_async_copy(grads_hbm.at[slot], grads.at[slot], sems.at[3, slot]),
            pltpu.make_async_copy(own_hbm.at[slot], own.at[slot], sems.at[4, slot]),
        )

    def stores(slot):
        return (
            pltpu.make_async_copy(out.at[slot], out_hbm.at[slot], sems.at[0, slot]),
            pltpu.make_async_copy(qgrad.at[slot], qgrad_hbm.at[slot], sems.at[1, slot]),
            pltpu.make_async_copy(own_grad.at[slot], own_grad_hbm.at[slot], sems.at[5, slot]),
        )

    @pl.loop(0, jnp.minimum(count, 2))
    def _(slot):
        for copy in loads(slot):
            copy.start()

    for group in range(GROUPS):
        filled[group] = 0

    @pl.loop(0, N_DP)
    def _(block):
        group = block_group[block]
        order[group * BLOCKS + filled[group]] = block
        filled[group] = filled[group] + 1

    accum[...] = jnp.zeros_like(accum)

    @pl.loop(count, SLOTS)
    def _(slot):
        out[slot] = jnp.zeros(out.shape[1:], BF16)
        qgrad[slot] = jnp.zeros(qgrad.shape[1:], BF16)
        own_grad[slot] = jnp.zeros(own_grad.shape[1:], BF16)
        for copy in stores(slot):
            copy.start()

    key_pos = lax.broadcasted_iota(jnp.int32, (RESP, RESP), 0)
    query_pos = lax.broadcasted_iota(jnp.int32, (RESP, RESP), 1)

    def columns(part):
        return slice(part * HD, (part + 1) * HD)

    def blocks_of(slot):
        group = slot_groups[slot, me]
        return [order[group * BLOCKS + j] for j in range(BLOCKS)]

    def keys_values(slot, head):
        ids, cols = blocks_of(slot), columns(head)
        ours = jnp.concatenate([near[i, :, cols] for i in ids], 0)
        theirs = jnp.concatenate([far[i, :, cols] for i in ids], 0)
        keys, values = jnp.where(first, ours, theirs), jnp.where(first, theirs, ours)
        return (
            jnp.concatenate([keys, own[slot, :, cols]], 0),
            jnp.concatenate([values, own[slot, :, columns(2 + head)]], 0),
        )

    def query_rows(slot, head):
        return jnp.concatenate(
            [queries[slot, :, columns(head * REPEATS + r)] for r in range(REPEATS)], 0
        )

    def softmax(slot, head):
        expd_ref, inverse_ref = states[head]
        keys, _ = keys_values(slot, head)
        scores = dot(keys, query_rows(slot, head), NT)
        yield
        visible = jnp.concatenate([key_pos <= query_pos] * REPEATS, 1)
        scores = jnp.concatenate(
            [scores[:prefix_rows], jnp.where(visible, scores[prefix_rows:], -1e30)], 0
        )
        top = jnp.max(scores, 0, keepdims=True)
        yield
        expd = jnp.exp2((scores - top) * LOG2_SCALE)
        expd_ref[...] = expd.astype(BF16)
        yield
        inverse_ref[...] = 1.0 / jnp.sum(expd, 0, keepdims=True)

    def gradients(slot, head):
        expd_ref, inverse_ref = states[head]
        keys, values = keys_values(slot, head)
        expd, inverse = expd_ref[...], inverse_ref[...]
        attended = dot(values.T, expd, NN) * inverse
        scaled = jnp.concatenate(
            [grads[slot, :, columns(head * REPEATS + r)].T for r in range(REPEATS)], 1
        )
        scaled = (scaled.astype(F32) * inverse).astype(BF16)
        yield
        delta = jnp.sum(scaled.astype(F32) * attended, 0, keepdims=True)
        dprob = dot(values, scaled, NN)
        yield
        dscore = expd * (dprob - delta).astype(BF16)
        value_grads = dot(expd, scaled, NT)
        yield
        query_grad = dot(keys.T, dscore, NN) * SCALE
        key_grads = dot(dscore, query_rows(slot, head), NN) * SCALE
        yield
        for r in range(REPEATS):
            rows = slice(r * RESP, (r + 1) * RESP)
            cols = columns(head * REPEATS + r)
            out[slot, :, cols] = attended[:, rows].T.astype(BF16)
            qgrad[slot, :, cols] = query_grad[:, rows].T.astype(BF16)
        for j, i in enumerate(blocks_of(slot)):
            rows = slice(j * RESP, (j + 1) * RESP)
            accum[i, :, columns(head)] += key_grads[rows]
            accum[i, :, columns(2 + head)] += value_grads[rows]
        own_grad[slot, :, columns(head)] = key_grads[prefix_rows:].astype(BF16)
        own_grad[slot, :, columns(2 + head)] = value_grads[prefix_rows:].astype(BF16)

    def together(*parts):
        parts = list(parts)
        while parts:
            parts = [part for part in parts if next(part, part) is None]

    @pl.when(count > 0)
    def _():
        for copy in loads(0):
            copy.wait()
        together(softmax(0, 0))

    @pl.loop(0, count)
    def _(slot):
        later = jnp.minimum(slot + 1, count - 1)

        @pl.when(slot + 2 < count)
        def _():
            for copy in loads(slot + 2):
                copy.start()

        @pl.when(later > slot)
        def _():
            for copy in loads(later):
                copy.wait()

        together(gradients(slot, 0), softmax(slot, 1))
        together(gradients(slot, 1), softmax(later, 0))
        for copy in stores(slot):
            copy.start()

    halves = []
    for place, (half, half_hbm, mine) in enumerate(
        (
            (send_k, send_k_hbm, 1 - core),
            (send_v, send_v_hbm, 1 - core),
            (keep_k, keep_k_hbm, core),
            (keep_v, keep_v_hbm, core),
        )
    ):
        cols = slice(place % 2 * 2 * HD, (place % 2 + 1) * 2 * HD)
        for part in range(4):
            chips = pl.ds(4 * part, 4)
            for chip in range(4 * part, 4 * part + 4):
                half[chip] = accum[2 * chip + mine, :, cols].astype(BF16)
            copy = pltpu.make_async_copy(
                half.at[chips], half_hbm.at[chips], sems.at[6 + place, part]
            )
            copy.start()
            halves.append(copy)

    @pl.loop(0, SLOTS)
    def _(slot):
        for copy in stores(slot):
            copy.wait()

    for copy in halves:
        copy.wait()


def after_kernel(*refs):
    del refs


def after(array, tokens, space):
    anywhere = pl.BlockSpec(memory_space=pl.ANY)
    spec = pl.BlockSpec(memory_space=space)
    return pl.pallas_call(
        after_kernel,
        in_specs=[spec] + [anywhere] * len(tokens),
        out_specs=spec,
        out_shape=space(array.shape, array.dtype),
        input_output_aliases={0: 0},
        compiler_params=pltpu.CompilerParams(vmem_limit_bytes=2**20),
        name="after",
    )(
        pltpu.with_memory_space_constraint(array, space),
        *tokens,
    )


def after_all(arrays, tokens):
    anywhere = pl.BlockSpec(memory_space=pl.ANY)
    return pl.pallas_call(
        after_kernel,
        in_specs=[anywhere] * (len(arrays) + len(tokens)),
        out_specs=[anywhere] * len(arrays),
        out_shape=[jax.ShapeDtypeStruct(array.shape, array.dtype) for array in arrays],
        input_output_aliases={i: i for i in range(len(arrays))},
        compiler_params=pltpu.CompilerParams(vmem_limit_bytes=2**20),
        name="after",
    )(*arrays, *tokens)


def columns_kernel(hidden, columns):
    share = hidden.shape[1] // N_DP
    for part in range(8):
        for y in range(4):
            start = (8 * y + part) * share
            columns[part, y * share : (y + 1) * share] = hidden[:, start : start + share].T


def columns_of(hidden):
    rows, width = hidden.shape
    return pl.pallas_call(
        columns_kernel,
        out_shape=jax.ShapeDtypeStruct((8, width // 8, rows), BF16),
        compiler_params=pltpu.CompilerParams(vmem_limit_bytes=8 * 2**20),
        name="columns",
    )(hidden)


def split_kernel(axis, keep, got, *parts):
    here = lax.axis_index(axis)
    for step, part in enumerate(parts):
        place = lax.rem(here + step, 4)
        for i in range(4):
            chip = place * 4 + i if axis == "y" else i * 4 + place
            part[i] = (keep[chip].astype(F32) + got[chip].astype(F32)).astype(BF16)


def split_sum(keep, got, axis):
    shape = (4,) + keep.shape[1:]
    return pl.pallas_call(
        functools.partial(split_kernel, axis),
        out_shape=[jax.ShapeDtypeStruct(shape, BF16)] * 4,
        compiler_params=pltpu.CompilerParams(vmem_limit_bytes=12 * 2**20),
        name="split",
    )(keep, got)


def reduce_kernel(axis, *refs):
    here = lax.axis_index(axis)
    for step in range(4):
        place = lax.rem(here + step, 4)
        total = refs[0][place].astype(F32)
        for ref in refs[1:4]:
            total = total + ref[place].astype(F32)
        refs[4 + step][...] = total.astype(BF16)


def reduce_of(parts, axis):
    return pl.pallas_call(
        functools.partial(reduce_kernel, axis),
        out_shape=[jax.ShapeDtypeStruct(parts[0].shape[1:], BF16)] * 4,
        compiler_params=pltpu.CompilerParams(vmem_limit_bytes=8 * 2**20),
        name="reduce",
    )(*parts)


def block_kernel(*refs):
    for half in range(2):
        total = refs[4 * half][...].astype(F32)
        for ref in refs[4 * half + 1 : 4 * half + 4]:
            total = total + ref[...].astype(F32)
        refs[8][:, half * 2 * HD : (half + 1) * 2 * HD] = total.astype(BF16)


def block_of(keys, values):
    return pl.pallas_call(
        block_kernel,
        out_shape=jax.ShapeDtypeStruct((keys[0].shape[0], 4 * HD), BF16),
        compiler_params=pltpu.CompilerParams(vmem_limit_bytes=8 * 2**20),
        name="block",
    )(*keys, *values)


def term_kernel(hidden, *refs):
    lines, others, parts, terms = refs[:4], refs[4:8], refs[8:12], refs[12]
    first = lax.axis_index("c") == 0
    here = lax.axis_index("z")
    total = None
    for step, (line, other) in enumerate(zip(lines, others)):
        z = lax.rem(here + 4 - step, 4)
        ours, theirs = line[...], other[...]
        pair = jnp.concatenate(
            [jnp.where(first, ours, theirs), jnp.where(first, theirs, ours)], 0
        )
        both = jnp.concatenate([hidden[2 * z], hidden[2 * z + 1]], 1)
        part = dot(both, pair, NN)
        total = part if total is None else total + part
    terms[...] = total
    share = parts[0].shape[0]
    here = lax.axis_index("y")
    for step, part in enumerate(parts):
        start = pl.multiple_of(lax.rem(here + step, 4) * share, share)
        part[...] = terms[pl.ds(start, share)].astype(BF16)


def term_of(hidden, lines, others):
    width, columns = hidden.shape[1], lines[0].shape[1]
    return pl.pallas_call(
        term_kernel,
        out_shape=[jax.ShapeDtypeStruct((width // 4, columns), BF16)] * 4,
        scratch_shapes=[pltpu.VMEM((width, columns), F32)],
        cost_estimate=pl.CostEstimate(
            flops=2000000000, bytes_accessed=10000000, transcendentals=0
        ),
        compiler_params=pltpu.CompilerParams(vmem_limit_bytes=12 * 2**20),
        name="term",
    )(hidden, *lines, *others)


def hold_kernel(source, target, sem):
    copy = pltpu.make_async_copy(source, target, sem)
    copy.start()
    copy.wait()


def hold(array):
    return pl.pallas_call(
        hold_kernel,
        in_specs=[pl.BlockSpec(memory_space=pl.ANY)],
        out_specs=pl.BlockSpec(memory_space=pltpu.VMEM),
        out_shape=pltpu.VMEM(array.shape, BF16),
        scratch_shapes=[pltpu.SemaphoreType.DMA],
        compiler_params=pltpu.CompilerParams(vmem_limit_bytes=2**20),
        name="hold",
    )(in_hbm(array))


def prompt_kernel(block, weight, *terms):
    here = lax.axis_index("x")
    rows = terms[0].shape[1]
    for step in (2, 1, 3, 0):
        start = pl.multiple_of(lax.rem(here + step, 4) * rows, rows)
        terms[step][...] = (
            dot(block[:, : 2 * HD], weight[0, pl.ds(start, rows)], NT)
            + dot(block[:, 2 * HD :], weight[1, pl.ds(start, rows)], NT)
        ).astype(BF16)


def prompt_terms(block, weight):
    shape = (block.shape[0], weight.shape[1] // 4)
    return pl.pallas_call(
        prompt_kernel,
        out_shape=[jax.ShapeDtypeStruct(shape, BF16)] * 4,
        in_specs=[pl.BlockSpec(memory_space=pltpu.VMEM)] * 2,
        cost_estimate=pl.CostEstimate(
            flops=8 * shape[0] * shape[1] * 4 * HD, bytes_accessed=2**22, transcendentals=0
        ),
        compiler_params=pltpu.CompilerParams(vmem_limit_bytes=16 * 2**20),
        name="prompt",
    )(block, pltpu.with_memory_space_constraint(weight, pltpu.VMEM))


def sum_kernel(*refs):
    *parts, result = refs
    total = None
    for part in parts:
        values = [part[i] for i in range(part.shape[0])] if part.ndim == 3 else [part[...]]
        for value in values:
            value = value.astype(F32)
            total = value if total is None else total + value
    result[...] = total.astype(result.dtype)


def sum_of(parts, dtype):
    return pl.pallas_call(
        sum_kernel,
        out_shape=jax.ShapeDtypeStruct(parts[0].shape[-2:], dtype),
        compiler_params=pltpu.CompilerParams(vmem_limit_bytes=8 * 2**20),
        name="sum",
    )(*parts)


def attention(pack_counts, slot_groups, block_group, queries, out_grad, own, near, far):
    vmem = pl.BlockSpec(memory_space=pltpu.VMEM)
    smem = pl.BlockSpec(memory_space=pltpu.SMEM)
    anywhere = pl.BlockSpec(memory_space=pl.ANY)
    rows = BLOCKS * RESP + RESP
    shared = (N_DP // 2, RESP, 2 * HD)
    outer = [in_hbm(array) for array in (queries, out_grad, own)]
    inner = [pltpu.with_memory_space_constraint(array, pltpu.VMEM) for array in (near, far)]
    return pl.pallas_call(
        attention_kernel,
        in_specs=[smem] * 3 + [anywhere] * 3 + [vmem] * 2,
        out_specs=[anywhere] * 7,
        out_shape=[
            pltpu.HBM(queries.shape, BF16),
            pltpu.HBM(queries.shape, BF16),
            pltpu.HBM(own.shape, BF16),
            *[pltpu.HBM(shared, BF16) for _ in range(4)],
        ],
        scratch_shapes=[pltpu.VMEM(queries.shape, BF16)] * 4
        + [pltpu.VMEM(own.shape, BF16)] * 2
        + [pltpu.VMEM(shared, BF16)] * 4
        + [
            pltpu.VMEM((N_DP, RESP, 4 * HD), F32),
            pltpu.VMEM((rows, REPEATS * RESP), BF16),
            pltpu.VMEM((rows, REPEATS * RESP), BF16),
            pltpu.VMEM((1, REPEATS * RESP), F32),
            pltpu.VMEM((1, REPEATS * RESP), F32),
            pltpu.SMEM((N_DP,), jnp.int32),
            pltpu.SMEM((GROUPS,), jnp.int32),
            pltpu.SemaphoreType.DMA((10, SLOTS)),
        ],
        cost_estimate=pl.CostEstimate(
            flops=6 * 2 * 2 * SLOTS * REPEATS * RESP * rows * HD,
            bytes_accessed=16 * 2**20,
            transcendentals=2 * SLOTS * REPEATS * RESP * rows,
        ),
        compiler_params=pltpu.CompilerParams(vmem_limit_bytes=40 * 2**20),
        name="attention",
    )(pack_counts, slot_groups.T, block_group, *outer, *inner)


def in_hbm(array):
    return pltpu.with_memory_space_constraint(array, pltpu.HBM)


def swap_cores(array):
    return lax.ppermute(array, "c", [(0, 1), (1, 0)])


def exchange(array, axes):
    return lax.all_to_all(array, axes, 0, 0, tiled=True)


def body(
    prompt_hidden, kv_weight, queries, out_grad, own_kv, pack_counts, slot_groups, block_group
):
    width = prompt_hidden.shape[1]
    core = lax.axis_index("c")
    first = core == 0

    projected = jnp.einsum(
        "pd,dkc->pkc", prompt_hidden, kv_weight, preferred_element_type=F32
    ).astype(BF16)

    keys, values = projected[:, 0], projected[:, 1]
    kept = jnp.where(first, keys, values)
    got = swap_cores(jnp.where(first, values, keys))
    piece = jnp.concatenate([jnp.where(first, kept, got), jnp.where(first, got, kept)], 0)
    piece = jnp.broadcast_to(piece[None], (16, 2 * RESP, 2 * HD))
    near = exchange(piece, ("y", "z")).reshape(N_DP, RESP, 2 * HD)

    own = own_kv.reshape(SLOTS, RESP, 4 * HD)
    columns = columns_of(prompt_hidden)
    relaid = kv_weight.transpose(1, 0, 2)
    near = after(near, (in_hbm(own), in_hbm(columns), in_hbm(relaid)), pltpu.VMEM)
    hidden_y = exchange(columns, ("z", "c"))

    outs, qgrads, own_grad, send_k, send_v, keep_k, keep_v = attention(
        pack_counts, slot_groups, block_group, queries, out_grad, own, near, swap_cores(near)
    )
    own_grad = own_grad.reshape(SLOTS, RESP, 2, 2 * HD)

    def ring(array, axis, step):
        return lax.ppermute(array, axis, [(i, (i + step) % 4) for i in range(4)])

    def deal(parts, axis):
        return [parts[0]] + [ring(parts[step], axis, step) for step in (1, 2, 3)]

    send_k = after(send_k, (hidden_y,), pltpu.HBM)
    keys = deal(split_sum(keep_k, swap_cores(send_k), "y"), "y")
    values = deal(split_sum(keep_v, swap_cores(send_v), "z"), "z")
    relaid = hold(after(relaid, (in_hbm(send_k),), pltpu.HBM))
    values[2] = after_all([values[2]], [relaid])[0]
    keys = deal(reduce_of(keys, "z"), "z")
    values = deal(reduce_of(values, "y"), "y")
    block_b = block_of(keys, values)

    terms = prompt_terms(block_b, relaid)
    prompt_grad = sum_of([terms[0], *[ring(terms[step], "x", step) for step in (2, 1, 3)]], BF16)

    lines = [block_b] + [ring(block_b, "z", step) for step in (1, 2, 3)]
    shares = term_of(hidden_y, lines, [swap_cores(line) for line in lines])
    moved = [ring(shares[step], "y", step) for step in (2, 1, 3)]
    weight_grad = sum_of([shares[0], *moved], F32)
    weight_grad = weight_grad.reshape(width // N_DP, 2, 2 * HD)
    return (outs, qgrads, own_grad, weight_grad, prompt_grad)


def solution(mesh):
    grid = Mesh(mesh.devices.reshape(4, 4, 2, 4), ("y", "z", "c", "x"))
    dp = ("y", "z", "c")
    return jax.shard_map(
        body,
        mesh=grid,
        in_specs=(
            P(dp, None),
            P(None, None, "x"),
            P(dp, None, "x"),
            P(dp, None, "x"),
            P(dp, None, None, "x"),
            P(),
            P(),
            P(),
        ),
        out_specs=(
            P(dp, None, "x"),
            P(dp, None, "x"),
            P(dp, None, None, "x"),
            P(dp, None, "x"),
            P(dp, "x"),
        ),
        check_vma=False,
    )
```

```python
import functools
import math

import jax
import jax.numpy as jnp
from jax import lax
from jax.experimental import pallas as pl
from jax.experimental.pallas import tpu as pltpu
from jax.sharding import Mesh, PartitionSpec as P

HD = 128
GROUP = 16
GROUPS = 8
BLOCKS = 4
SLOTS = 8
RESP = 128
REPEATS = 5
N_DP = 32
F32 = jnp.float32
BF16 = jnp.bfloat16
SCALE = 1.0 / math.sqrt(HD)
LOG2_SCALE = SCALE * math.log2(math.e)
NT = (((1,), (1,)), ((), ()))
NN = (((1,), (0,)), ((), ()))


def dot(a, b, dims):
    return lax.dot_general(a, b, dims, preferred_element_type=F32)


def attention_kernel(
    pack_counts, slot_groups, block_group, queries_hbm, grads_hbm, own_hbm, near, far,
    out_hbm, qgrad_hbm, own_grad_hbm, send_k_hbm, send_v_hbm, keep_k_hbm, keep_v_hbm,
    queries, grads, out, qgrad, own, own_grad, send_k, send_v, keep_k, keep_v, accum,
    expd_0, expd_1, inverse_0, inverse_1, order, filled, sems,
):
    core = lax.axis_index("c")
    me = (lax.axis_index("y") * 4 + lax.axis_index("z")) * 2 + core
    count = pack_counts[me]
    first = core == 0
    prefix_rows = BLOCKS * RESP
    states = ((expd_0, inverse_0), (expd_1, inverse_1))

    def loads(slot):
        return (
            pltpu.make_async_copy(queries_hbm.at[slot], queries.at[slot], sems.at[2, slot]),
            pltpu.make_async_copy(grads_hbm.at[slot], grads.at[slot], sems.at[3, slot]),
            pltpu.make_async_copy(own_hbm.at[slot], own.at[slot], sems.at[4, slot]),
        )

    def stores(slot):
        return (
            pltpu.make_async_copy(out.at[slot], out_hbm.at[slot], sems.at[0, slot]),
            pltpu.make_async_copy(qgrad.at[slot], qgrad_hbm.at[slot], sems.at[1, slot]),
            pltpu.make_async_copy(own_grad.at[slot], own_grad_hbm.at[slot], sems.at[5, slot]),
        )

    @pl.loop(0, jnp.minimum(count, 2))
    def _(slot):
        for copy in loads(slot):
            copy.start()

    for group in range(GROUPS):
        filled[group] = 0

    @pl.loop(0, N_DP)
    def _(block):
        group = block_group[block]
        order[group * BLOCKS + filled[group]] = block
        filled[group] = filled[group] + 1

    accum[...] = jnp.zeros_like(accum)

    @pl.loop(count, SLOTS)
    def _(slot):
        out[slot] = jnp.zeros(out.shape[1:], BF16)
        qgrad[slot] = jnp.zeros(qgrad.shape[1:], BF16)
        own_grad[slot] = jnp.zeros(own_grad.shape[1:], BF16)
        for copy in stores(slot):
            copy.start()

    key_pos = lax.broadcasted_iota(jnp.int32, (RESP, RESP), 0)
    query_pos = lax.broadcasted_iota(jnp.int32, (RESP, RESP), 1)

    def columns(part):
        return slice(part * HD, (part + 1) * HD)

    def blocks_of(slot):
        group = slot_groups[slot, me]
        return [order[group * BLOCKS + j] for j in range(BLOCKS)]

    def keys_values(slot, head):
        ids, cols = blocks_of(slot), columns(head)
        ours = jnp.concatenate([near[i, :, cols] for i in ids], 0)
        theirs = jnp.concatenate([far[i, :, cols] for i in ids], 0)
        keys, values = jnp.where(first, ours, theirs), jnp.where(first, theirs, ours)
        return (
            jnp.concatenate([keys, own[slot, :, cols]], 0),
            jnp.concatenate([values, own[slot, :, columns(2 + head)]], 0),
        )

    def query_rows(slot, head):
        return jnp.concatenate(
            [queries[slot, :, columns(head * REPEATS + r)] for r in range(REPEATS)], 0
        )

    def softmax(slot, head):
        expd_ref, inverse_ref = states[head]
        keys, _ = keys_values(slot, head)
        scores = dot(keys, query_rows(slot, head), NT)
        yield
        visible = jnp.concatenate([key_pos <= query_pos] * REPEATS, 1)
        scores = jnp.concatenate(
            [scores[:prefix_rows], jnp.where(visible, scores[prefix_rows:], -1e30)], 0
        )
        top = jnp.max(scores, 0, keepdims=True)
        yield
        expd = jnp.exp2((scores - top) * LOG2_SCALE)
        expd_ref[...] = expd.astype(BF16)
        yield
        inverse_ref[...] = 1.0 / jnp.sum(expd, 0, keepdims=True)

    def gradients(slot, head):
        expd_ref, inverse_ref = states[head]
        keys, values = keys_values(slot, head)
        expd, inverse = expd_ref[...], inverse_ref[...]
        attended = dot(values.T, expd, NN) * inverse
        scaled = jnp.concatenate(
            [grads[slot, :, columns(head * REPEATS + r)].T for r in range(REPEATS)], 1
        )
        scaled = (scaled.astype(F32) * inverse).astype(BF16)
        yield
        delta = jnp.sum(scaled.astype(F32) * attended, 0, keepdims=True)
        dprob = dot(values, scaled, NN)
        yield
        dscore = expd * (dprob - delta).astype(BF16)
        value_grads = dot(expd, scaled, NT)
        yield
        query_grad = dot(keys.T, dscore, NN) * SCALE
        key_grads = dot(dscore, query_rows(slot, head), NN) * SCALE
        yield
        for r in range(REPEATS):
            rows = slice(r * RESP, (r + 1) * RESP)
            cols = columns(head * REPEATS + r)
            out[slot, :, cols] = attended[:, rows].T.astype(BF16)
            qgrad[slot, :, cols] = query_grad[:, rows].T.astype(BF16)
        for j, i in enumerate(blocks_of(slot)):
            rows = slice(j * RESP, (j + 1) * RESP)
            accum[i, :, columns(head)] += key_grads[rows]
            accum[i, :, columns(2 + head)] += value_grads[rows]
        own_grad[slot, :, columns(head)] = key_grads[prefix_rows:].astype(BF16)
        own_grad[slot, :, columns(2 + head)] = value_grads[prefix_rows:].astype(BF16)

    def together(*parts):
        parts = list(parts)
        while parts:
            parts = [part for part in parts if next(part, part) is None]

    @pl.when(count > 0)
    def _():
        for copy in loads(0):
            copy.wait()
        together(softmax(0, 0))

    @pl.loop(0, count)
    def _(slot):
        later = jnp.minimum(slot + 1, count - 1)

        @pl.when(slot + 2 < count)
        def _():
            for copy in loads(slot + 2):
                copy.start()

        @pl.when(later > slot)
        def _():
            for copy in loads(later):
                copy.wait()

        together(softmax(slot, 1))
        together(gradients(slot, 0))
        together(softmax(later, 0))
        together(gradients(slot, 1))
        for copy in stores(slot):
            copy.start()

    halves = []
    for place, (half, half_hbm, mine) in enumerate(
        (
            (send_k, send_k_hbm, 1 - core),
            (send_v, send_v_hbm, 1 - core),
            (keep_k, keep_k_hbm, core),
            (keep_v, keep_v_hbm, core),
        )
    ):
        cols = slice(place % 2 * 2 * HD, (place % 2 + 1) * 2 * HD)
        for part in range(4):
            chips = pl.ds(4 * part, 4)
            for chip in range(4 * part, 4 * part + 4):
                half[chip] = accum[2 * chip + mine, :, cols].astype(BF16)
            copy = pltpu.make_async_copy(
                half.at[chips], half_hbm.at[chips], sems.at[6 + place, part]
            )
            copy.start()
            halves.append(copy)

    @pl.loop(0, SLOTS)
    def _(slot):
        for copy in stores(slot):
            copy.wait()

    for copy in halves:
        copy.wait()


def after_kernel(*refs):
    del refs


def after(array, tokens, space):
    anywhere = pl.BlockSpec(memory_space=pl.ANY)
    spec = pl.BlockSpec(memory_space=space)
    return pl.pallas_call(
        after_kernel,
        in_specs=[spec] + [anywhere] * len(tokens),
        out_specs=spec,
        out_shape=space(array.shape, array.dtype),
        input_output_aliases={0: 0},
        compiler_params=pltpu.CompilerParams(vmem_limit_bytes=2**20),
        name="after",
    )(
        pltpu.with_memory_space_constraint(array, space),
        *tokens,
    )


def after_all(arrays, tokens):
    anywhere = pl.BlockSpec(memory_space=pl.ANY)
    return pl.pallas_call(
        after_kernel,
        in_specs=[anywhere] * (len(arrays) + len(tokens)),
        out_specs=[anywhere] * len(arrays),
        out_shape=[jax.ShapeDtypeStruct(array.shape, array.dtype) for array in arrays],
        input_output_aliases={i: i for i in range(len(arrays))},
        compiler_params=pltpu.CompilerParams(vmem_limit_bytes=2**20),
        name="after",
    )(*arrays, *tokens)


def columns_kernel(hidden, columns):
    share = hidden.shape[1] // N_DP
    for part in range(8):
        for y in range(4):
            start = (8 * y + part) * share
            columns[part, y * share : (y + 1) * share] = hidden[:, start : start + share].T


def columns_of(hidden):
    rows, width = hidden.shape
    return pl.pallas_call(
        columns_kernel,
        out_shape=jax.ShapeDtypeStruct((8, width // 8, rows), BF16),
        compiler_params=pltpu.CompilerParams(vmem_limit_bytes=8 * 2**20),
        name="columns",
    )(hidden)


def split_kernel(axis, keep, got, *parts):
    here = lax.axis_index(axis)
    for step, part in enumerate(parts):
        place = lax.rem(here + step, 4)
        for i in range(4):
            chip = place * 4 + i if axis == "y" else i * 4 + place
            part[i] = (keep[chip].astype(F32) + got[chip].astype(F32)).astype(BF16)


def split_sum(keep, got, axis):
    shape = (4,) + keep.shape[1:]
    return pl.pallas_call(
        functools.partial(split_kernel, axis),
        out_shape=[jax.ShapeDtypeStruct(shape, BF16)] * 4,
        compiler_params=pltpu.CompilerParams(vmem_limit_bytes=12 * 2**20),
        name="split",
    )(keep, got)


def reduce_kernel(axis, *refs):
    here = lax.axis_index(axis)
    for step in range(4):
        place = lax.rem(here + step, 4)
        total = refs[0][place].astype(F32)
        for ref in refs[1:4]:
            total = total + ref[place].astype(F32)
        refs[4 + step][...] = total.astype(BF16)


def reduce_of(parts, axis):
    return pl.pallas_call(
        functools.partial(reduce_kernel, axis),
        out_shape=[jax.ShapeDtypeStruct(parts[0].shape[1:], BF16)] * 4,
        compiler_params=pltpu.CompilerParams(vmem_limit_bytes=8 * 2**20),
        name="reduce",
    )(*parts)


def block_kernel(*refs):
    for half in range(2):
        total = refs[4 * half][...].astype(F32)
        for ref in refs[4 * half + 1 : 4 * half + 4]:
            total = total + ref[...].astype(F32)
        refs[8][:, half * 2 * HD : (half + 1) * 2 * HD] = total.astype(BF16)


def block_of(keys, values):
    return pl.pallas_call(
        block_kernel,
        out_shape=jax.ShapeDtypeStruct((keys[0].shape[0], 4 * HD), BF16),
        compiler_params=pltpu.CompilerParams(vmem_limit_bytes=8 * 2**20),
        name="block",
    )(*keys, *values)


def term_kernel(hidden, *refs):
    lines, others, parts, terms = refs[:4], refs[4:8], refs[8:12], refs[12]
    first = lax.axis_index("c") == 0
    here = lax.axis_index("z")
    total = None
    for step, (line, other) in enumerate(zip(lines, others)):
        z = lax.rem(here + 4 - step, 4)
        ours, theirs = line[...], other[...]
        pair = jnp.concatenate(
            [jnp.where(first, ours, theirs), jnp.where(first, theirs, ours)], 0
        )
        both = jnp.concatenate([hidden[2 * z], hidden[2 * z + 1]], 1)
        part = dot(both, pair, NN)
        total = part if total is None else total + part
    terms[...] = total
    share = parts[0].shape[0]
    here = lax.axis_index("y")
    for step, part in enumerate(parts):
        start = pl.multiple_of(lax.rem(here + step, 4) * share, share)
        part[...] = terms[pl.ds(start, share)].astype(BF16)


def term_of(hidden, lines, others):
    width, columns = hidden.shape[1], lines[0].shape[1]
    return pl.pallas_call(
        term_kernel,
        out_shape=[jax.ShapeDtypeStruct((width // 4, columns), BF16)] * 4,
        scratch_shapes=[pltpu.VMEM((width, columns), F32)],
        cost_estimate=pl.CostEstimate(
            flops=2000000000, bytes_accessed=10000000, transcendentals=0
        ),
        compiler_params=pltpu.CompilerParams(vmem_limit_bytes=12 * 2**20),
        name="term",
    )(hidden, *lines, *others)


def hold_kernel(source, target, sem):
    copy = pltpu.make_async_copy(source, target, sem)
    copy.start()
    copy.wait()


def hold(array):
    return pl.pallas_call(
        hold_kernel,
        in_specs=[pl.BlockSpec(memory_space=pl.ANY)],
        out_specs=pl.BlockSpec(memory_space=pltpu.VMEM),
        out_shape=pltpu.VMEM(array.shape, BF16),
        scratch_shapes=[pltpu.SemaphoreType.DMA],
        compiler_params=pltpu.CompilerParams(vmem_limit_bytes=2**20),
        name="hold",
    )(in_hbm(array))


def prompt_kernel(block, weight, *terms):
    here = lax.axis_index("x")
    rows = terms[0].shape[1]
    for step in (2, 1, 3, 0):
        start = pl.multiple_of(lax.rem(here + step, 4) * rows, rows)
        terms[step][...] = (
            dot(block[:, : 2 * HD], weight[0, pl.ds(start, rows)], NT)
            + dot(block[:, 2 * HD :], weight[1, pl.ds(start, rows)], NT)
        ).astype(BF16)


def prompt_terms(block, weight):
    shape = (block.shape[0], weight.shape[1] // 4)
    return pl.pallas_call(
        prompt_kernel,
        out_shape=[jax.ShapeDtypeStruct(shape, BF16)] * 4,
        in_specs=[pl.BlockSpec(memory_space=pltpu.VMEM)] * 2,
        cost_estimate=pl.CostEstimate(
            flops=8 * shape[0] * shape[1] * 4 * HD, bytes_accessed=2**22, transcendentals=0
        ),
        compiler_params=pltpu.CompilerParams(vmem_limit_bytes=16 * 2**20),
        name="prompt",
    )(block, pltpu.with_memory_space_constraint(weight, pltpu.VMEM))


def sum_kernel(*refs):
    *parts, result = refs
    total = None
    for part in parts:
        values = [part[i] for i in range(part.shape[0])] if part.ndim == 3 else [part[...]]
        for value in values:
            value = value.astype(F32)
            total = value if total is None else total + value
    result[...] = total.astype(result.dtype)


def sum_of(parts, dtype):
    return pl.pallas_call(
        sum_kernel,
        out_shape=jax.ShapeDtypeStruct(parts[0].shape[-2:], dtype),
        compiler_params=pltpu.CompilerParams(vmem_limit_bytes=8 * 2**20),
        name="sum",
    )(*parts)


def attention(pack_counts, slot_groups, block_group, queries, out_grad, own, near, far):
    vmem = pl.BlockSpec(memory_space=pltpu.VMEM)
    smem = pl.BlockSpec(memory_space=pltpu.SMEM)
    anywhere = pl.BlockSpec(memory_space=pl.ANY)
    rows = BLOCKS * RESP + RESP
    shared = (N_DP // 2, RESP, 2 * HD)
    outer = [in_hbm(array) for array in (queries, out_grad, own)]
    inner = [pltpu.with_memory_space_constraint(array, pltpu.VMEM) for array in (near, far)]
    return pl.pallas_call(
        attention_kernel,
        in_specs=[smem] * 3 + [anywhere] * 3 + [vmem] * 2,
        out_specs=[anywhere] * 7,
        out_shape=[
            pltpu.HBM(queries.shape, BF16),
            pltpu.HBM(queries.shape, BF16),
            pltpu.HBM(own.shape, BF16),
            *[pltpu.HBM(shared, BF16) for _ in range(4)],
        ],
        scratch_shapes=[pltpu.VMEM(queries.shape, BF16)] * 4
        + [pltpu.VMEM(own.shape, BF16)] * 2
        + [pltpu.VMEM(shared, BF16)] * 4
        + [
            pltpu.VMEM((N_DP, RESP, 4 * HD), F32),
            pltpu.VMEM((rows, REPEATS * RESP), BF16),
            pltpu.VMEM((rows, REPEATS * RESP), BF16),
            pltpu.VMEM((1, REPEATS * RESP), F32),
            pltpu.VMEM((1, REPEATS * RESP), F32),
            pltpu.SMEM((N_DP,), jnp.int32),
            pltpu.SMEM((GROUPS,), jnp.int32),
            pltpu.SemaphoreType.DMA((10, SLOTS)),
        ],
        cost_estimate=pl.CostEstimate(
            flops=6 * 2 * 2 * SLOTS * REPEATS * RESP * rows * HD,
            bytes_accessed=16 * 2**20,
            transcendentals=2 * SLOTS * REPEATS * RESP * rows,
        ),
        compiler_params=pltpu.CompilerParams(vmem_limit_bytes=40 * 2**20),
        name="attention",
    )(pack_counts, slot_groups.T, block_group, *outer, *inner)


def in_hbm(array):
    return pltpu.with_memory_space_constraint(array, pltpu.HBM)


def swap_cores(array):
    return lax.ppermute(array, "c", [(0, 1), (1, 0)])


def exchange(array, axes):
    return lax.all_to_all(array, axes, 0, 0, tiled=True)


def body(
    prompt_hidden, kv_weight, queries, out_grad, own_kv, pack_counts, slot_groups, block_group
):
    width = prompt_hidden.shape[1]
    core = lax.axis_index("c")
    first = core == 0

    projected = jnp.einsum(
        "pd,dkc->pkc", prompt_hidden, kv_weight, preferred_element_type=F32
    ).astype(BF16)

    keys, values = projected[:, 0], projected[:, 1]
    kept = jnp.where(first, keys, values)
    got = swap_cores(jnp.where(first, values, keys))
    piece = jnp.concatenate([jnp.where(first, kept, got), jnp.where(first, got, kept)], 0)
    piece = jnp.broadcast_to(piece[None], (16, 2 * RESP, 2 * HD))
    near = exchange(piece, ("y", "z")).reshape(N_DP, RESP, 2 * HD)

    own = own_kv.reshape(SLOTS, RESP, 4 * HD)
    columns = columns_of(prompt_hidden)
    relaid = kv_weight.transpose(1, 0, 2)
    near = after(near, (in_hbm(own), in_hbm(columns), in_hbm(relaid)), pltpu.VMEM)
    hidden_y = exchange(columns, ("z", "c"))

    outs, qgrads, own_grad, send_k, send_v, keep_k, keep_v = attention(
        pack_counts, slot_groups, block_group, queries, out_grad, own, near, swap_cores(near)
    )
    own_grad = own_grad.reshape(SLOTS, RESP, 2, 2 * HD)

    def ring(array, axis, step):
        return lax.ppermute(array, axis, [(i, (i + step) % 4) for i in range(4)])

    def deal(parts, axis):
        return [parts[0]] + [ring(parts[step], axis, step) for step in (1, 2, 3)]

    send_k = after(send_k, (hidden_y,), pltpu.HBM)
    keys = deal(split_sum(keep_k, swap_cores(send_k), "y"), "y")
    values = deal(split_sum(keep_v, swap_cores(send_v), "z"), "z")
    relaid = hold(after(relaid, (in_hbm(send_k),), pltpu.HBM))
    values[2] = after_all([values[2]], [relaid])[0]
    keys = deal(reduce_of(keys, "z"), "z")
    values = deal(reduce_of(values, "y"), "y")
    block_b = block_of(keys, values)

    terms = prompt_terms(block_b, relaid)
    prompt_grad = sum_of([terms[0], *[ring(terms[step], "x", step) for step in (2, 1, 3)]], BF16)

    lines = [block_b] + [ring(block_b, "z", step) for step in (1, 2, 3)]
    shares = term_of(hidden_y, lines, [swap_cores(line) for line in lines])
    moved = [ring(shares[step], "y", step) for step in (2, 1, 3)]
    weight_grad = sum_of([shares[0], *moved], F32)
    weight_grad = weight_grad.reshape(width // N_DP, 2, 2 * HD)
    return (outs, qgrads, own_grad, weight_grad, prompt_grad)


def solution(mesh):
    grid = Mesh(mesh.devices.reshape(4, 4, 2, 4), ("y", "z", "c", "x"))
    dp = ("y", "z", "c")
    return jax.shard_map(
        body,
        mesh=grid,
        in_specs=(
            P(dp, None),
            P(None, None, "x"),
            P(dp, None, "x"),
            P(dp, None, "x"),
            P(dp, None, None, "x"),
            P(),
            P(),
            P(),
        ),
        out_specs=(
            P(dp, None, "x"),
            P(dp, None, "x"),
            P(dp, None, None, "x"),
            P(dp, None, "x"),
            P(dp, "x"),
        ),
        check_vma=False,
    )
```

```python
import functools
import math

import jax
import jax.numpy as jnp
from jax import lax
from jax.experimental import pallas as pl
from jax.experimental.pallas import tpu as pltpu
from jax.sharding import Mesh, PartitionSpec as P

HD = 128
GROUP = 16
GROUPS = 8
BLOCKS = 4
SLOTS = 8
RESP = 128
REPEATS = 5
N_DP = 32
F32 = jnp.float32
BF16 = jnp.bfloat16
SCALE = 1.0 / math.sqrt(HD)
LOG2_SCALE = SCALE * math.log2(math.e)
NT = (((1,), (1,)), ((), ()))
NN = (((1,), (0,)), ((), ()))


def dot(a, b, dims):
    return lax.dot_general(a, b, dims, preferred_element_type=F32)


def attention_kernel(
    pack_counts, slot_groups, block_group, queries_hbm, grads_hbm, own_hbm, near, far,
    out_hbm, qgrad_hbm, own_grad_hbm, send_k_hbm, send_v_hbm, keep_k_hbm, keep_v_hbm,
    queries, grads, out, qgrad, own, own_grad, send_k, send_v, keep_k, keep_v, accum,
    expd_0, expd_1, inverse_0, inverse_1, order, filled, sems,
):
    core = lax.axis_index("c")
    me = (lax.axis_index("y") * 4 + lax.axis_index("z")) * 2 + core
    count = pack_counts[me]
    first = core == 0
    prefix_rows = BLOCKS * RESP
    states = ((expd_0, inverse_0), (expd_1, inverse_1))

    def loads(slot):
        return (
            pltpu.make_async_copy(queries_hbm.at[slot], queries.at[slot], sems.at[2, slot]),
            pltpu.make_async_copy(grads_hbm.at[slot], grads.at[slot], sems.at[3, slot]),
            pltpu.make_async_copy(own_hbm.at[slot], own.at[slot], sems.at[4, slot]),
        )

    def stores(slot):
        return (
            pltpu.make_async_copy(out.at[slot], out_hbm.at[slot], sems.at[0, slot]),
            pltpu.make_async_copy(qgrad.at[slot], qgrad_hbm.at[slot], sems.at[1, slot]),
            pltpu.make_async_copy(own_grad.at[slot], own_grad_hbm.at[slot], sems.at[5, slot]),
        )

    @pl.loop(0, jnp.minimum(count, 2))
    def _(slot):
        for copy in loads(slot):
            copy.start()

    for group in range(GROUPS):
        filled[group] = 0

    @pl.loop(0, N_DP)
    def _(block):
        group = block_group[block]
        order[group * BLOCKS + filled[group]] = block
        filled[group] = filled[group] + 1

    accum[...] = jnp.zeros_like(accum)

    @pl.loop(count, SLOTS)
    def _(slot):
        out[slot] = jnp.zeros(out.shape[1:], BF16)
        qgrad[slot] = jnp.zeros(qgrad.shape[1:], BF16)
        own_grad[slot] = jnp.zeros(own_grad.shape[1:], BF16)
        for copy in stores(slot):
            copy.start()

    key_pos = lax.broadcasted_iota(jnp.int32, (RESP, RESP), 0)
    query_pos = lax.broadcasted_iota(jnp.int32, (RESP, RESP), 1)

    def columns(part):
        return slice(part * HD, (part + 1) * HD)

    def blocks_of(slot):
        group = slot_groups[slot, me]
        return [order[group * BLOCKS + j] for j in range(BLOCKS)]

    def keys_values(slot, head):
        ids, cols = blocks_of(slot), columns(head)
        ours = jnp.concatenate([near[i, :, cols] for i in ids], 0)
        theirs = jnp.concatenate([far[i, :, cols] for i in ids], 0)
        keys, values = jnp.where(first, ours, theirs), jnp.where(first, theirs, ours)
        return (
            jnp.concatenate([keys, own[slot, :, cols]], 0),
            jnp.concatenate([values, own[slot, :, columns(2 + head)]], 0),
        )

    def query_rows(slot, head):
        return jnp.concatenate(
            [queries[slot, :, columns(head * REPEATS + r)] for r in range(REPEATS)], 0
        )

    def softmax(slot, head):
        expd_ref, inverse_ref = states[head]
        keys, _ = keys_values(slot, head)
        scores = dot(keys, query_rows(slot, head), NT)
        yield
        visible = jnp.concatenate([key_pos <= query_pos] * REPEATS, 1)
        scores = jnp.concatenate(
            [scores[:prefix_rows], jnp.where(visible, scores[prefix_rows:], -1e30)], 0
        )
        top = jnp.max(scores, 0, keepdims=True)
        yield
        expd = jnp.exp2((scores - top) * LOG2_SCALE)
        expd_ref[...] = expd.astype(BF16)
        yield
        inverse_ref[...] = 1.0 / jnp.sum(expd, 0, keepdims=True)

    def gradients(slot, head):
        expd_ref, inverse_ref = states[head]
        keys, values = keys_values(slot, head)
        expd, inverse = expd_ref[...], inverse_ref[...]
        attended = dot(values.T, expd, NN) * inverse
        scaled = jnp.concatenate(
            [grads[slot, :, columns(head * REPEATS + r)].T for r in range(REPEATS)], 1
        )
        scaled = (scaled.astype(F32) * inverse).astype(BF16)
        yield
        delta = jnp.sum(scaled.astype(F32) * attended, 0, keepdims=True)
        dprob = dot(values, scaled, NN)
        yield
        dscore = expd * (dprob - delta).astype(BF16)
        value_grads = dot(expd, scaled, NT)
        yield
        query_grad = dot(keys.T, dscore, NN) * SCALE
        key_grads = dot(dscore, query_rows(slot, head), NN) * SCALE
        yield
        for r in range(REPEATS):
            rows = slice(r * RESP, (r + 1) * RESP)
            cols = columns(head * REPEATS + r)
            out[slot, :, cols] = attended[:, rows].T.astype(BF16)
            qgrad[slot, :, cols] = query_grad[:, rows].T.astype(BF16)
        for j, i in enumerate(blocks_of(slot)):
            rows = slice(j * RESP, (j + 1) * RESP)
            accum[i, :, columns(head)] += key_grads[rows]
            accum[i, :, columns(2 + head)] += value_grads[rows]
        own_grad[slot, :, columns(head)] = key_grads[prefix_rows:].astype(BF16)
        own_grad[slot, :, columns(2 + head)] = value_grads[prefix_rows:].astype(BF16)

    def together(*parts):
        parts = list(parts)
        while parts:
            parts = [part for part in parts if next(part, part) is None]

    @pl.when(count > 0)
    def _():
        for copy in loads(0):
            copy.wait()
        together(softmax(0, 0))

    @pl.loop(0, count)
    def _(slot):
        later = jnp.minimum(slot + 1, count - 1)

        @pl.when(slot + 2 < count)
        def _():
            for copy in loads(slot + 2):
                copy.start()

        together(softmax(slot, 1))
        together(gradients(slot, 0))

        @pl.when(later > slot)
        def _():
            for copy in loads(later):
                copy.wait()
            together(softmax(later, 0))

        together(gradients(slot, 1))
        for copy in stores(slot):
            copy.start()

    halves = []
    for place, (half, half_hbm, mine) in enumerate(
        (
            (send_k, send_k_hbm, 1 - core),
            (send_v, send_v_hbm, 1 - core),
            (keep_k, keep_k_hbm, core),
            (keep_v, keep_v_hbm, core),
        )
    ):
        cols = slice(place % 2 * 2 * HD, (place % 2 + 1) * 2 * HD)
        for part in range(4):
            chips = pl.ds(4 * part, 4)
            for chip in range(4 * part, 4 * part + 4):
                half[chip] = accum[2 * chip + mine, :, cols].astype(BF16)
            copy = pltpu.make_async_copy(
                half.at[chips], half_hbm.at[chips], sems.at[6 + place, part]
            )
            copy.start()
            halves.append(copy)

    @pl.loop(0, SLOTS)
    def _(slot):
        for copy in stores(slot):
            copy.wait()

    for copy in halves:
        copy.wait()


def after_kernel(*refs):
    del refs


def after(array, tokens, space):
    anywhere = pl.BlockSpec(memory_space=pl.ANY)
    spec = pl.BlockSpec(memory_space=space)
    return pl.pallas_call(
        after_kernel,
        in_specs=[spec] + [anywhere] * len(tokens),
        out_specs=spec,
        out_shape=space(array.shape, array.dtype),
        input_output_aliases={0: 0},
        compiler_params=pltpu.CompilerParams(vmem_limit_bytes=2**20),
        name="after",
    )(
        pltpu.with_memory_space_constraint(array, space),
        *tokens,
    )


def after_all(arrays, tokens):
    anywhere = pl.BlockSpec(memory_space=pl.ANY)
    return pl.pallas_call(
        after_kernel,
        in_specs=[anywhere] * (len(arrays) + len(tokens)),
        out_specs=[anywhere] * len(arrays),
        out_shape=[jax.ShapeDtypeStruct(array.shape, array.dtype) for array in arrays],
        input_output_aliases={i: i for i in range(len(arrays))},
        compiler_params=pltpu.CompilerParams(vmem_limit_bytes=2**20),
        name="after",
    )(*arrays, *tokens)


def columns_kernel(hidden, columns):
    share = hidden.shape[1] // N_DP
    for part in range(8):
        for y in range(4):
            start = (8 * y + part) * share
            columns[part, y * share : (y + 1) * share] = hidden[:, start : start + share].T


def columns_of(hidden):
    rows, width = hidden.shape
    return pl.pallas_call(
        columns_kernel,
        out_shape=jax.ShapeDtypeStruct((8, width // 8, rows), BF16),
        compiler_params=pltpu.CompilerParams(vmem_limit_bytes=8 * 2**20),
        name="columns",
    )(hidden)


def split_kernel(axis, keep, got, *parts):
    here = lax.axis_index(axis)
    for step, part in enumerate(parts):
        place = lax.rem(here + step, 4)
        for i in range(4):
            chip = place * 4 + i if axis == "y" else i * 4 + place
            part[i] = (keep[chip].astype(F32) + got[chip].astype(F32)).astype(BF16)


def split_sum(keep, got, axis):
    shape = (4,) + keep.shape[1:]
    return pl.pallas_call(
        functools.partial(split_kernel, axis),
        out_shape=[jax.ShapeDtypeStruct(shape, BF16)] * 4,
        compiler_params=pltpu.CompilerParams(vmem_limit_bytes=12 * 2**20),
        name="split",
    )(keep, got)


def reduce_kernel(axis, *refs):
    here = lax.axis_index(axis)
    for step in range(4):
        place = lax.rem(here + step, 4)
        total = refs[0][place].astype(F32)
        for ref in refs[1:4]:
            total = total + ref[place].astype(F32)
        refs[4 + step][...] = total.astype(BF16)


def reduce_of(parts, axis):
    return pl.pallas_call(
        functools.partial(reduce_kernel, axis),
        out_shape=[jax.ShapeDtypeStruct(parts[0].shape[1:], BF16)] * 4,
        compiler_params=pltpu.CompilerParams(vmem_limit_bytes=8 * 2**20),
        name="reduce",
    )(*parts)


def block_kernel(*refs):
    for half in range(2):
        total = refs[4 * half][...].astype(F32)
        for ref in refs[4 * half + 1 : 4 * half + 4]:
            total = total + ref[...].astype(F32)
        refs[8][:, half * 2 * HD : (half + 1) * 2 * HD] = total.astype(BF16)


def block_of(keys, values):
    return pl.pallas_call(
        block_kernel,
        out_shape=jax.ShapeDtypeStruct((keys[0].shape[0], 4 * HD), BF16),
        compiler_params=pltpu.CompilerParams(vmem_limit_bytes=8 * 2**20),
        name="block",
    )(*keys, *values)


def term_kernel(hidden, *refs):
    lines, others, parts, terms = refs[:4], refs[4:8], refs[8:12], refs[12]
    first = lax.axis_index("c") == 0
    here = lax.axis_index("z")
    total = None
    for step, (line, other) in enumerate(zip(lines, others)):
        z = lax.rem(here + 4 - step, 4)
        ours, theirs = line[...], other[...]
        pair = jnp.concatenate(
            [jnp.where(first, ours, theirs), jnp.where(first, theirs, ours)], 0
        )
        both = jnp.concatenate([hidden[2 * z], hidden[2 * z + 1]], 1)
        part = dot(both, pair, NN)
        total = part if total is None else total + part
    terms[...] = total
    share = parts[0].shape[0]
    here = lax.axis_index("y")
    for step, part in enumerate(parts):
        start = pl.multiple_of(lax.rem(here + step, 4) * share, share)
        part[...] = terms[pl.ds(start, share)].astype(BF16)


def term_of(hidden, lines, others):
    width, columns = hidden.shape[1], lines[0].shape[1]
    return pl.pallas_call(
        term_kernel,
        out_shape=[jax.ShapeDtypeStruct((width // 4, columns), BF16)] * 4,
        scratch_shapes=[pltpu.VMEM((width, columns), F32)],
        cost_estimate=pl.CostEstimate(
            flops=2000000000, bytes_accessed=10000000, transcendentals=0
        ),
        compiler_params=pltpu.CompilerParams(vmem_limit_bytes=12 * 2**20),
        name="term",
    )(hidden, *lines, *others)


def hold_kernel(source, target, sem):
    copy = pltpu.make_async_copy(source, target, sem)
    copy.start()
    copy.wait()


def hold(array):
    return pl.pallas_call(
        hold_kernel,
        in_specs=[pl.BlockSpec(memory_space=pl.ANY)],
        out_specs=pl.BlockSpec(memory_space=pltpu.VMEM),
        out_shape=pltpu.VMEM(array.shape, BF16),
        scratch_shapes=[pltpu.SemaphoreType.DMA],
        compiler_params=pltpu.CompilerParams(vmem_limit_bytes=2**20),
        name="hold",
    )(in_hbm(array))


def prompt_kernel(block, weight, *terms):
    here = lax.axis_index("x")
    rows = terms[0].shape[1]
    for step in (2, 1, 3, 0):
        start = pl.multiple_of(lax.rem(here + step, 4) * rows, rows)
        terms[step][...] = (
            dot(block[:, : 2 * HD], weight[0, pl.ds(start, rows)], NT)
            + dot(block[:, 2 * HD :], weight[1, pl.ds(start, rows)], NT)
        ).astype(BF16)


def prompt_terms(block, weight):
    shape = (block.shape[0], weight.shape[1] // 4)
    return pl.pallas_call(
        prompt_kernel,
        out_shape=[jax.ShapeDtypeStruct(shape, BF16)] * 4,
        in_specs=[pl.BlockSpec(memory_space=pltpu.VMEM)] * 2,
        cost_estimate=pl.CostEstimate(
            flops=8 * shape[0] * shape[1] * 4 * HD, bytes_accessed=2**22, transcendentals=0
        ),
        compiler_params=pltpu.CompilerParams(vmem_limit_bytes=16 * 2**20),
        name="prompt",
    )(block, pltpu.with_memory_space_constraint(weight, pltpu.VMEM))


def sum_kernel(*refs):
    *parts, result = refs
    total = None
    for part in parts:
        values = [part[i] for i in range(part.shape[0])] if part.ndim == 3 else [part[...]]
        for value in values:
            value = value.astype(F32)
            total = value if total is None else total + value
    result[...] = total.astype(result.dtype)


def sum_of(parts, dtype):
    return pl.pallas_call(
        sum_kernel,
        out_shape=jax.ShapeDtypeStruct(parts[0].shape[-2:], dtype),
        compiler_params=pltpu.CompilerParams(vmem_limit_bytes=8 * 2**20),
        name="sum",
    )(*parts)


def attention(pack_counts, slot_groups, block_group, queries, out_grad, own, near, far):
    vmem = pl.BlockSpec(memory_space=pltpu.VMEM)
    smem = pl.BlockSpec(memory_space=pltpu.SMEM)
    anywhere = pl.BlockSpec(memory_space=pl.ANY)
    rows = BLOCKS * RESP + RESP
    shared = (N_DP // 2, RESP, 2 * HD)
    outer = [in_hbm(array) for array in (queries, out_grad, own)]
    inner = [pltpu.with_memory_space_constraint(array, pltpu.VMEM) for array in (near, far)]
    return pl.pallas_call(
        attention_kernel,
        in_specs=[smem] * 3 + [anywhere] * 3 + [vmem] * 2,
        out_specs=[anywhere] * 7,
        out_shape=[
            pltpu.HBM(queries.shape, BF16),
            pltpu.HBM(queries.shape, BF16),
            pltpu.HBM(own.shape, BF16),
            *[pltpu.HBM(shared, BF16) for _ in range(4)],
        ],
        scratch_shapes=[pltpu.VMEM(queries.shape, BF16)] * 4
        + [pltpu.VMEM(own.shape, BF16)] * 2
        + [pltpu.VMEM(shared, BF16)] * 4
        + [
            pltpu.VMEM((N_DP, RESP, 4 * HD), F32),
            pltpu.VMEM((rows, REPEATS * RESP), BF16),
            pltpu.VMEM((rows, REPEATS * RESP), BF16),
            pltpu.VMEM((1, REPEATS * RESP), F32),
            pltpu.VMEM((1, REPEATS * RESP), F32),
            pltpu.SMEM((N_DP,), jnp.int32),
            pltpu.SMEM((GROUPS,), jnp.int32),
            pltpu.SemaphoreType.DMA((10, SLOTS)),
        ],
        cost_estimate=pl.CostEstimate(
            flops=6 * 2 * 2 * SLOTS * REPEATS * RESP * rows * HD,
            bytes_accessed=16 * 2**20,
            transcendentals=2 * SLOTS * REPEATS * RESP * rows,
        ),
        compiler_params=pltpu.CompilerParams(vmem_limit_bytes=40 * 2**20),
        name="attention",
    )(pack_counts, slot_groups.T, block_group, *outer, *inner)


def in_hbm(array):
    return pltpu.with_memory_space_constraint(array, pltpu.HBM)


def swap_cores(array):
    return lax.ppermute(array, "c", [(0, 1), (1, 0)])


def exchange(array, axes):
    return lax.all_to_all(array, axes, 0, 0, tiled=True)


def body(
    prompt_hidden, kv_weight, queries, out_grad, own_kv, pack_counts, slot_groups, block_group
):
    width = prompt_hidden.shape[1]
    core = lax.axis_index("c")
    first = core == 0

    projected = jnp.einsum(
        "pd,dkc->pkc", prompt_hidden, kv_weight, preferred_element_type=F32
    ).astype(BF16)

    keys, values = projected[:, 0], projected[:, 1]
    kept = jnp.where(first, keys, values)
    got = swap_cores(jnp.where(first, values, keys))
    piece = jnp.concatenate([jnp.where(first, kept, got), jnp.where(first, got, kept)], 0)
    piece = jnp.broadcast_to(piece[None], (16, 2 * RESP, 2 * HD))
    near = exchange(piece, ("y", "z")).reshape(N_DP, RESP, 2 * HD)

    own = own_kv.reshape(SLOTS, RESP, 4 * HD)
    columns = columns_of(prompt_hidden)
    relaid = kv_weight.transpose(1, 0, 2)
    near = after(near, (in_hbm(own), in_hbm(columns), in_hbm(relaid)), pltpu.VMEM)
    hidden_y = exchange(columns, ("z", "c"))

    outs, qgrads, own_grad, send_k, send_v, keep_k, keep_v = attention(
        pack_counts, slot_groups, block_group, queries, out_grad, own, near, swap_cores(near)
    )
    own_grad = own_grad.reshape(SLOTS, RESP, 2, 2 * HD)

    def ring(array, axis, step):
        return lax.ppermute(array, axis, [(i, (i + step) % 4) for i in range(4)])

    def deal(parts, axis):
        return [parts[0]] + [ring(parts[step], axis, step) for step in (1, 2, 3)]

    send_k = after(send_k, (hidden_y,), pltpu.HBM)
    keys = deal(split_sum(keep_k, swap_cores(send_k), "y"), "y")
    values = deal(split_sum(keep_v, swap_cores(send_v), "z"), "z")
    relaid = hold(after(relaid, (in_hbm(send_k),), pltpu.HBM))
    values[2] = after_all([values[2]], [relaid])[0]
    keys = deal(reduce_of(keys, "z"), "z")
    values = deal(reduce_of(values, "y"), "y")
    block_b = block_of(keys, values)

    terms = prompt_terms(block_b, relaid)
    prompt_grad = sum_of([terms[0], *[ring(terms[step], "x", step) for step in (2, 1, 3)]], BF16)

    lines = [block_b] + [ring(block_b, "z", step) for step in (1, 2, 3)]
    shares = term_of(hidden_y, lines, [swap_cores(line) for line in lines])
    moved = [ring(shares[step], "y", step) for step in (2, 1, 3)]
    weight_grad = sum_of([shares[0], *moved], F32)
    weight_grad = weight_grad.reshape(width // N_DP, 2, 2 * HD)
    return (outs, qgrads, own_grad, weight_grad, prompt_grad)


def solution(mesh):
    grid = Mesh(mesh.devices.reshape(4, 4, 2, 4), ("y", "z", "c", "x"))
    dp = ("y", "z", "c")
    return jax.shard_map(
        body,
        mesh=grid,
        in_specs=(
            P(dp, None),
            P(None, None, "x"),
            P(dp, None, "x"),
            P(dp, None, "x"),
            P(dp, None, None, "x"),
            P(),
            P(),
            P(),
        ),
        out_specs=(
            P(dp, None, "x"),
            P(dp, None, "x"),
            P(dp, None, None, "x"),
            P(dp, None, "x"),
            P(dp, "x"),
        ),
        check_vma=False,
    )
```
